512 devices in a mesh: pts: 128 (over x, z, core), scene: 4 (over y).
Axes of the slice: x: 4, y: 4, z: 16, core: 2. Of those that a mesh axis runs over, the one named last changes fastest.
Arguments:
- points: bfloat16 [4, 16384, 512], P('scene', 'pts'), may hold values from -6 to 6
- cotangent: bfloat16 [4, 16384, 512], P('scene', 'pts'), may hold values from -6 to 6
- valid_counts: int32 [4, 16], P('scene'), may hold values from 256 to 1024, as said below
- zorder_targets: int32 [4, 16384], P('scene', 'pts'), may hold values from 0 to 16383, as said below
- hilbert_sources: int32 [4, 16384], P('scene', 'pts'), may hold values from 0 to 16383, as said below
- zorder_project: bfloat16 [512, 1536], P('pts')
- zorder_output: bfloat16 [512, 512], P('pts'), may hold values from -0.25 to 0.25
- hilbert_project: bfloat16 [512, 1536], P('pts')
- hilbert_output: bfloat16 [512, 512], P('pts'), may hold values from -0.25 to 0.25
Outputs:
- point_grads: bfloat16 [4, 16384, 512], P('scene', 'pts')
- output_grad: float32 [512, 512], P('pts')
The draws below stay inside these ranges and needn't reach their ends.
Inputs may be any that keep to these rules, and one draw needn't show every extreme that they name: `valid_counts`: every scene has a patch with 1024 valid points and one with 256. `hilbert_sources`: for each scene, a permutation of all blocks; zorder_targets is its inverse. Index u of pts holds Z-order blocks u * 128 to (u + 1) * 128 - 1 and Hilbert positions likewise. The blocks that index u sends to index v number at most 2, and this number depends only on v - u modulo the size of pts; 2 is reached. `zorder_targets`: the inverse permutation of hilbert_sources in each scene.
All inputs are finite; a program needn't handle non-finite values.
Results may differ from the reference program's by a relative error of at most 0.034.
The reference program's roundings to bfloat16 on the way count: a program that leaves them out, or rounds other values in their place, can miss the bound.
Values may be sent and summed in bfloat16 or wider, within the bound.
No kernel may reach another device: no remote copies, remote signals or barrier semaphores. Data moves between devices by JAX's collectives and lax.ppermute only.
A program may use at most 64 MiB of HBM per device.

```python
import jax
import jax.numpy as jnp
from jax import lax

WIDTH = 512
HEADS = 16
PATCH = 1024
BLOCKS = 128
BLOCK_ROWS = 1
ROOM = 2
SCENES = 4
POINTS = 16384
ZPATCHES = 16
BLOCKS_ALL = 16384


def projection(key):
    values = jnp.clip(jax.random.normal(key, (WIDTH, 3 * WIDTH), jnp.float32), -6.0, 6.0) * WIDTH ** (-0.5)
    columns = jnp.arange(3 * WIDTH)
    return jnp.where(columns[None, :] < 2 * WIDTH, values, values)


def draw_zorder_project(key, part):
    key = jax.random.fold_in(key, 3)
    return projection(key).astype(jnp.bfloat16)


def draw_hilbert_project(key, part):
    key = jax.random.fold_in(key, 7)
    return projection(key).astype(jnp.bfloat16)


def block_lists(key):
    devices = BLOCKS_ALL // BLOCKS
    sources_all = []
    targets_all = []
    for scene in range(SCENES):
        scene_key = jax.random.fold_in(key, 1000 + scene)
        first_key, mix_key, order_key, noise_key = jax.random.split(scene_key, 4)
        favored = jax.random.randint(first_key, (), 0, devices).astype(jnp.int32)
        others = (favored + 1 + jnp.arange((devices - 1) * ROOM, dtype=jnp.int32) % (devices - 1)) % devices
        others = jax.random.permutation(mix_key, others)[:BLOCKS - ROOM]
        offsets = jnp.concatenate([jnp.zeros((ROOM,), jnp.int32) + favored, others])
        shuffled = jax.vmap(lambda single: jax.random.permutation(single, offsets))(jax.random.split(order_key, devices))
        owners = (jnp.arange(devices, dtype=jnp.int32)[:, None] + shuffled) % devices
        noise = jax.random.permutation(noise_key, BLOCKS_ALL).astype(jnp.int32)
        scores = owners.reshape(BLOCKS_ALL) * BLOCKS_ALL + noise
        sources = jnp.argsort(scores).astype(jnp.int32)
        targets = jnp.argsort(sources).astype(jnp.int32)
        sources_all.append(sources)
        targets_all.append(targets)
    return (jnp.stack(sources_all), jnp.stack(targets_all))


def draw_hilbert_sources(key, part):
    return block_lists(key)[0]


def draw_zorder_targets(key, part):
    return block_lists(key)[1]


def draw_valid_counts(key, part):
    key = jax.random.fold_in(key, 17)
    count_key, full_key, least_key = jax.random.split(key, 3)
    counts = jax.random.randint(count_key, (SCENES, ZPATCHES), PATCH // 4, PATCH + 1).astype(jnp.int32)
    full_at = jax.random.randint(full_key, (SCENES,), 0, ZPATCHES)
    least_at = (full_at + 1 + jax.random.randint(least_key, (SCENES,), 0, ZPATCHES - 1)) % ZPATCHES
    scene_ids = jnp.arange(SCENES)
    counts = counts.at[scene_ids, full_at].set(PATCH)
    counts = counts.at[scene_ids, least_at].set(PATCH // 4)
    return counts.astype(jnp.int32)


def block_levels(key, extent, cuts, low, high):
    def one(dim, parts):
        heights = jax.random.uniform(jax.random.fold_in(jax.random.fold_in(key, 6), dim), (parts,), jnp.float32, low / len(cuts), high / len(cuts))
        return jnp.repeat(jnp.exp(heights), extent[dim] // parts).reshape((-1,) + (1,) * (len(extent) - dim - 1))

    factor_of = one(*cuts[0])
    for cut in cuts[1:]:
        factor_of = factor_of * one(*cut)
    return factor_of


def gaussian(key, extent, width, limit, pieces=(), held_as=jnp.bfloat16):
    drawn = jax.random.normal(key, extent, jnp.float32) * width
    if len(pieces) > 0:
        drawn = block_levels(key, extent, pieces, -0.22, 0.18) * drawn
    return jnp.clip(drawn, min=-limit, max=limit).astype(held_as)


def setup_inputs(seed: int = 0) -> dict:
    key_list = jax.random.split(jax.random.key(seed), 10)
    points = gaussian(key_list[0], (SCENES, POINTS, WIDTH), 1.0, 6.0, ((0, 4), (1, 128)))
    cotangent = gaussian(key_list[1], (SCENES, POINTS, WIDTH), 1.0, 6.0, ((0, 4), (1, 128)))
    valid_counts = draw_valid_counts(jax.random.fold_in(key_list[9], 71), 0)
    zorder_targets = draw_zorder_targets(jax.random.fold_in(key_list[9], 71), 0)
    hilbert_sources = draw_hilbert_sources(jax.random.fold_in(key_list[9], 71), 0)
    zorder_project = draw_zorder_project(jax.random.fold_in(key_list[9], 71), 0)
    zorder_output = gaussian(key_list[6], (WIDTH, WIDTH), WIDTH ** -0.5, 0.25, ((0, 128),))
    hilbert_project = draw_hilbert_project(jax.random.fold_in(key_list[9], 71), 0)
    hilbert_output = gaussian(key_list[8], (WIDTH, WIDTH), WIDTH ** -0.5, 0.25, ((0, 128),))
    return dict(points=points, cotangent=cotangent, valid_counts=valid_counts, zorder_targets=zorder_targets, hilbert_sources=hilbert_sources, zorder_project=zorder_project, zorder_output=zorder_output, hilbert_project=hilbert_project, hilbert_output=hilbert_output)


EPSILON = 1e-05
NEGATIVE = -1e+30

def normalize(rows_in):
    values = rows_in.astype(jnp.float32)
    center = values - lax.optimization_barrier(jnp.mean(values, axis=-1, keepdims=True))
    inverse = lax.rsqrt(lax.optimization_barrier(jnp.mean(center * center, axis=-1, keepdims=True)) + EPSILON)
    return (center * inverse, inverse)

def normalize_back(grad_normed, unit, inverse):
    middle = grad_normed - lax.optimization_barrier(jnp.mean(grad_normed, axis=-1, keepdims=True))
    return inverse * (middle - unit * lax.optimization_barrier(jnp.mean(grad_normed * unit, axis=-1, keepdims=True)))

def split_heads(values):
    return values.astype(jnp.float32).reshape(values.shape[0], HEADS, WIDTH // HEADS)

def rounded(values):
    return lax.optimization_barrier(values.astype(jnp.bfloat16)).astype(jnp.float32)

def patch_probs(query, keys, key_ok, scaling):
    scores = jnp.einsum('qhd,khd->hqk', query, keys) * scaling
    scores = jnp.where(key_ok[None, None, :], scores, NEGATIVE)
    highest = lax.optimization_barrier(jnp.max(scores, axis=2, keepdims=True))
    weights = jnp.exp(scores - highest)
    return weights / lax.optimization_barrier(jnp.sum(weights, axis=2, keepdims=True))

def patch_forward(projected, key_ok):
    query = split_heads(projected[:, :WIDTH])
    keys = split_heads(projected[:, WIDTH:2 * WIDTH])
    values = split_heads(projected[:, 2 * WIDTH:])
    scaling = (WIDTH // HEADS) ** (-0.5)
    probs_low = rounded(patch_probs(query, keys, key_ok, scaling))
    attended = jnp.einsum('hqk,khd->qhd', probs_low, values)
    return attended.astype(jnp.bfloat16).reshape(projected.shape[0], WIDTH)

def patch_backward(projected, key_ok, grad_attended):
    row_count = projected.shape[0]
    query = split_heads(projected[:, :WIDTH])
    keys = split_heads(projected[:, WIDTH:2 * WIDTH])
    values = split_heads(projected[:, 2 * WIDTH:])
    scaling = (WIDTH // HEADS) ** (-0.5)
    probs = patch_probs(query, keys, key_ok, scaling)
    probs_low = rounded(probs)
    grad_heads = split_heads(grad_attended)
    grad_probs = jnp.einsum('qhd,khd->hqk', grad_heads, values)
    grad_values = jnp.einsum('hqk,qhd->khd', probs_low, grad_heads)
    row_dot = lax.optimization_barrier(jnp.sum(probs * grad_probs, axis=2, keepdims=True))
    grad_scores = rounded(probs * (grad_probs - row_dot))
    grad_query = jnp.einsum('hqk,khd->qhd', grad_scores, keys) * scaling
    grad_keys = jnp.einsum('hqk,qhd->khd', grad_scores, query) * scaling
    attended = jnp.einsum('hqk,khd->qhd', probs_low, values).astype(jnp.bfloat16).reshape(row_count, WIDTH)
    grad_projected = jnp.concatenate([grad_query.reshape(row_count, WIDTH), grad_keys.reshape(row_count, WIDTH), grad_values.reshape(row_count, WIDTH)], axis=1).astype(jnp.bfloat16)
    return (grad_projected, attended)

def sublayer_forward(rows_in, flags, project, output):
    unit, inverse = normalize(rows_in)
    projected = jnp.dot(unit.astype(jnp.bfloat16), project, preferred_element_type=jnp.float32).astype(jnp.bfloat16)
    attended = lax.map(lambda item: patch_forward(item[0], item[1]), (projected.reshape(-1, PATCH, 3 * WIDTH), flags.reshape(-1, PATCH)))
    return (rows_in.astype(jnp.float32) + jnp.dot(attended.reshape(-1, WIDTH), output, preferred_element_type=jnp.float32)).astype(jnp.bfloat16)

def sublayer_backward(rows_in, flags, project, output, grads):
    unit, inverse = normalize(rows_in)
    projected = jnp.dot(unit.astype(jnp.bfloat16), project, preferred_element_type=jnp.float32).astype(jnp.bfloat16)
    grad_attended = jnp.dot(grads, output.T, preferred_element_type=jnp.float32).astype(jnp.bfloat16)
    patch_grads, attended = lax.map(lambda item: patch_backward(item[0], item[1], item[2]), (projected.reshape(-1, PATCH, 3 * WIDTH), flags.reshape(-1, PATCH), grad_attended.reshape(-1, PATCH, WIDTH)))
    grad_projected = patch_grads.reshape(-1, 3 * WIDTH)
    grad_normed = jnp.dot(grad_projected, project.T, preferred_element_type=jnp.float32)
    grad_rows = (grads.astype(jnp.float32) + normalize_back(grad_normed, unit, inverse)).astype(jnp.bfloat16)
    weight_term = jnp.dot(attended.reshape(-1, WIDTH).T, grads, preferred_element_type=jnp.float32)
    return (grad_rows, weight_term)

def reference(points, cotangent, valid_counts, zorder_targets, hilbert_sources, zorder_project, zorder_output, hilbert_project, hilbert_output):
    offsets = jnp.arange(BLOCK_ROWS, dtype=jnp.int32)
    point_ids = jnp.arange(POINTS, dtype=jnp.int32)

    def one_scene(running, item):
        scene_rows, scene_grads, counts, targets, sources = item
        flags = point_ids % PATCH < counts[point_ids // PATCH]
        mixed = sublayer_forward(scene_rows, flags, zorder_project, zorder_output)
        hilbert_order = (sources[:, None] * BLOCK_ROWS + offsets[None, :]).reshape(POINTS)
        back_order = (targets[:, None] * BLOCK_ROWS + offsets[None, :]).reshape(POINTS)
        grad_hilbert, weight_term = sublayer_backward(mixed[hilbert_order], flags[hilbert_order], hilbert_project, hilbert_output, scene_grads[hilbert_order])
        grad_rows, unused = sublayer_backward(scene_rows, flags, zorder_project, zorder_output, grad_hilbert[back_order])
        return (running + weight_term, grad_rows)
    running, point_grads = lax.scan(one_scene, jnp.zeros((WIDTH, WIDTH), jnp.float32), (points, cotangent, valid_counts, zorder_targets, hilbert_sources))
    return (point_grads, running * (SCENES * POINTS) ** (-0.5))
```

```python
import functools

import jax
import jax.numpy as jnp
from jax import lax
from jax.experimental import pallas as pl
from jax.experimental.pallas import tpu as pltpu
from jax.sharding import Mesh, PartitionSpec as P

HEADS = 16
PATCH = 1024
WIDTH = 512
HEAD = 32
ROWS = 128
PAIR = 64
MEMBERS = 8
PATCHES = 16
SLOTS = 16
META = 16
EPSILON = 1e-05
NEGATIVE = -1e30
SCALE = HEAD ** (-0.5)
LOG2E = 1.4426950408889634
QBLOCK = 256

F32 = jnp.float32
BF16 = jnp.bfloat16
PTS = ("x", "zh", "zl", "core")
GROUP = ("zl", "core")
ACROSS = ("x", "zh")


def dot(a, b, ca=1, cb=0):
    return lax.dot_general(a, b, (((ca,), (cb,)), ((), ())), preferred_element_type=F32)


def normalize(values):
    center = values - jnp.mean(values, axis=1, keepdims=True)
    inverse = lax.rsqrt(jnp.mean(center * center, axis=1, keepdims=True) + EPSILON)
    return center * inverse, inverse


def normalize_back(grad, unit, inverse):
    middle = grad - jnp.mean(grad, axis=1, keepdims=True)
    return inverse * (middle - unit * jnp.mean(grad * unit, axis=1, keepdims=True))


def iota(shape, dim):
    return lax.broadcasted_iota(jnp.int32, shape, dim)


def call(kernel, outs, scratch=(), smem=1, count=1):
    def run(*args):
        specs = [pl.BlockSpec(memory_space=pltpu.SMEM)] * smem
        specs += [pl.BlockSpec(memory_space=pltpu.VMEM)] * (len(args) - smem)
        return pl.pallas_call(
            kernel,
            out_shape=[jax.ShapeDtypeStruct(s, d) for s, d in outs],
            in_specs=specs,
            out_specs=[pl.BlockSpec(memory_space=pltpu.VMEM)] * len(outs),
            scratch_shapes=list(scratch),
            compiler_params=pltpu.CompilerParams(vmem_limit_bytes=48 * 1024 * 1024),
        )(*args)

    return run


def softmax_keys(keys, query, mask):
    scores = dot(keys, query, 1, 1) * (SCALE * LOG2E)
    scores = jnp.where(mask, scores, NEGATIVE)
    weights = jnp.exp2(scores - jnp.max(scores, axis=0, keepdims=True))
    return weights * (1.0 / jnp.sum(weights, axis=0, keepdims=True))


def wide(mask_ref):
    mask = mask_ref[...]
    return jnp.concatenate([mask] * (QBLOCK // ROWS), axis=1) > 0.5


def forward_kernel(scal, near, far, weights, qkv, attended, spread, mask_z, mask_h, att):
    member = scal[0]
    limit = scal[2 + scal[1]]
    w = weights[...]
    stride = ROWS + META
    device = iota((ROWS, ROWS), 0)
    total = jnp.zeros((ROWS, ROWS), F32)
    flagged = jnp.zeros((ROWS, ROWS), F32)
    bound = jnp.concatenate(
        [scal[2 + k] - ROWS * iota((MEMBERS, ROWS), 0) for k in range(PATCHES)], axis=0
    ).astype(F32)
    device_f = device.astype(F32)
    for b in range(MEMBERS):
        source = near if b % 2 == 0 else far
        first = (b // 2) * stride
        block = source[first : first + ROWS, :]
        unit, _ = normalize(block.astype(F32))
        qkv[b * ROWS : (b + 1) * ROWS, :] = dot(unit.astype(BF16), w).astype(BF16)
        index = iota((ROWS, ROWS), 0) + ROWS * jnp.bitwise_xor(member, b)
        mask_z[b * ROWS : (b + 1) * ROWS, :] = jnp.where(index < limit, 1.0, 0.0)
        meta = source[first + ROWS : first + stride, :].astype(F32)
        owner = meta[0:1, 0:ROWS]
        place = meta[0:1, ROWS : 2 * ROWS]
        hit = device_f == owner
        total += jnp.where(hit, 1.0, 0.0)
        flagged += jnp.where(hit & (place < bound), 1.0, 0.0)
    total = jnp.sum(total, axis=1, keepdims=True)
    flagged = jnp.sum(flagged, axis=1, keepdims=True)
    lane = iota((MEMBERS, ROWS), 1).astype(F32)
    mine = iota((MEMBERS, 1), 0) == member
    slot = iota((SLOTS, ROWS), 0).astype(F32)
    lane_slot = iota((SLOTS, ROWS), 1).astype(F32)
    offset = jnp.zeros((MEMBERS, 1), F32)
    flags = jnp.zeros((MEMBERS, ROWS), F32)
    for k in range(PATCHES):
        here = total[k * MEMBERS : (k + 1) * MEMBERS, :]
        good = flagged[k * MEMBERS : (k + 1) * MEMBERS, :]
        flags += jnp.where((lane >= offset) & (lane < offset + good), 1.0, 0.0)
        own_first = jnp.sum(jnp.where(mine, offset, 0.0), axis=0, keepdims=True)
        own_count = jnp.sum(jnp.where(mine, here, 0.0), axis=0, keepdims=True)
        spread[k * SLOTS : (k + 1) * SLOTS, :] = jnp.where(
            (slot + own_first == lane_slot) & (slot < own_count), 1.0, 0.0
        ).astype(BF16)
        offset += here
    flags = flags.astype(BF16)
    for b in range(MEMBERS):
        pick = jnp.where(iota((MEMBERS, ROWS), 0) == b, 1.0, 0.0).astype(BF16)
        mask_h[b * ROWS : (b + 1) * ROWS, :] = dot(flags, pick, 0, 0)
    mask = wide(mask_z)
    for h in range(2):
        keys = qkv[:, h * HEAD : (h + 1) * HEAD]
        values_t = qkv[:, PAIR + h * HEAD : PAIR + (h + 1) * HEAD].astype(F32).T.astype(BF16)
        for n in range(PATCH // QBLOCK):
            span = slice(n * QBLOCK, (n + 1) * QBLOCK)
            query = qkv[span, 2 * PAIR + h * HEAD : 2 * PAIR + (h + 1) * HEAD]
            probs = softmax_keys(keys, query, mask)
            att[h * HEAD : (h + 1) * HEAD, span] = dot(values_t, probs.astype(BF16))
    for b in range(MEMBERS):
        attended[jnp.bitwise_xor(member, b)] = att[:, b * ROWS : (b + 1) * ROWS].astype(BF16)


def mix_kernel(scal, targets_row, targets_col, attended, points, cotangent, output, send, placing):
    patch_row = targets_row[...] // PATCH
    patch_col = targets_col[...] // PATCH
    same = (patch_col == patch_row) & (iota((ROWS, ROWS), 0) < iota((ROWS, ROWS), 1))
    rank = jnp.sum(jnp.where(same, 1.0, 0.0), axis=0, keepdims=True).astype(jnp.int32)
    code = patch_row * SLOTS + rank
    place = jnp.where(iota((PATCHES * SLOTS, ROWS), 0) == code, 1.0, 0.0).astype(BF16)
    placing[...] = place
    mixed = points[...].astype(F32) + dot(attended[...], output[...], 0, 0)
    send[:, :WIDTH] = dot(place, mixed.astype(BF16)).astype(BF16)
    send[:, WIDTH:] = dot(place, cotangent[...]).astype(BF16)


def project_kernel(scal, arrived, spread, project, output, send, rows, grads):
    gathered = dot(spread[...], arrived[...], 0, 0).astype(BF16)
    mixed = gathered[:, :WIDTH]
    grad = gathered[:, WIDTH:]
    rows[...] = mixed
    grads[...] = grad
    unit, _ = normalize(mixed.astype(F32))
    projected = dot(unit.astype(BF16), project[...])
    grad_attended = dot(grad, output[...], 1, 1)
    for k in range(MEMBERS):
        send[k, :ROWS, :] = projected[:, WIDTH + k * ROWS : WIDTH + (k + 1) * ROWS].astype(BF16)
        cols = slice(k * PAIR, (k + 1) * PAIR)
        send[k, ROWS:, :] = jnp.concatenate(
            [projected[:, cols], grad_attended[:, cols]], axis=1
        ).astype(BF16)


def backward_body(member, qkv, grad_t, mask, send, attended, dq, dk, dv):
    for h in range(2):
        low, high = h * HEAD, (h + 1) * HEAD
        keys = qkv[:, low:high]
        values = qkv[:, PAIR + low : PAIR + high]
        keys_t = keys.astype(F32).T.astype(BF16)
        values_t = values.astype(F32).T.astype(BF16)
        for n in range(PATCH // QBLOCK):
            span = slice(n * QBLOCK, (n + 1) * QBLOCK)
            query = qkv[span, 2 * PAIR + low : 2 * PAIR + high]
            grad = grad_t[low:high, span]
            probs = softmax_keys(keys, query, mask)
            probs_low = probs.astype(BF16)
            grad_probs = dot(values, grad)
            row_dot = jnp.sum(probs * grad_probs, axis=0, keepdims=True)
            grad_scores = (probs * (grad_probs - row_dot)).astype(BF16)
            dq[low:high, span] = dot(keys_t, grad_scores)
            part_k = dot(grad_scores, query)
            part_v = dot(probs_low, grad, 1, 1)
            if n == 0:
                dk[:, low:high] = part_k
                dv[:, low:high] = part_v
            else:
                dk[:, low:high] += part_k
                dv[:, low:high] += part_v
            if attended is not None:
                attended[low:high, span] = dot(values_t, probs_low).astype(BF16)
    for b in range(MEMBERS):
        rows = slice(b * ROWS, (b + 1) * ROWS)
        dest = b if member is None else jnp.bitwise_xor(member, b)
        send[dest, :ROWS, :] = jnp.concatenate([dk[rows, :] * SCALE, dv[rows, :]], axis=1).astype(BF16)
        send[dest, ROWS:, :] = (dq[:, rows] * SCALE).astype(BF16)


def backward_h_kernel(scal, arrived, mask_h, send, attended, qkv, grad_t, dq, dk, dv):
    for b in range(MEMBERS):
        rows = slice(b * ROWS, (b + 1) * ROWS)
        qkv[rows, :ROWS] = arrived[b, :ROWS, :]
        both = arrived[b, ROWS:, :]
        qkv[rows, ROWS:] = both
        grad_t[:, rows] = both.astype(F32).T[PAIR:, :].astype(BF16)
    backward_body(None, qkv, grad_t, wide(mask_h), send, attended, dq, dk, dv)


def backward_z_kernel(scal, arrived, qkv, mask_z, send, grad_t, dq, dk, dv):
    member = scal[0]
    for b in range(MEMBERS):
        grad_t[:, b * ROWS : (b + 1) * ROWS] = arrived[jnp.bitwise_xor(member, b)]
    backward_body(member, qkv, grad_t, wide(mask_z), send, None, dq, dk, dv)


def input_grad(arrived, project, rows, grads):
    parts = [arrived[k, ROWS:, :].astype(F32) for k in range(MEMBERS)]
    query_part = jnp.concatenate(parts, axis=0).T.astype(BF16)
    grad_projected = jnp.concatenate(
        [query_part] + [arrived[k, :ROWS, :] for k in range(MEMBERS)], axis=1
    )
    grad_normed = dot(grad_projected, project[...], 1, 1)
    unit, inverse = normalize(rows[...].astype(F32))
    return (grads[...].astype(F32) + normalize_back(grad_normed, unit, inverse)).astype(BF16)


def return_kernel(scal, arrived, project, rows, grads, spread, send):
    grad = input_grad(arrived, project, rows, grads)
    send[...] = dot(spread[...], grad).astype(BF16)


def regain_kernel(scal, arrived, placing, output, grad_mixed, send):
    grad = dot(placing[...], arrived[...], 0, 0).astype(BF16)
    grad_mixed[...] = grad
    send[...] = dot(output[...], grad, 1, 1).astype(BF16)


def finish_kernel(scal, arrived, project, rows, grads, out):
    out[...] = input_grad(arrived, project, rows, grads)


def head_pairs(project):
    rows = project.shape[0]
    keys = project[:, WIDTH : 2 * WIDTH].reshape(rows, MEMBERS, PAIR)
    values = project[:, 2 * WIDTH :].reshape(rows, MEMBERS, PAIR)
    both = jnp.concatenate([keys, values], axis=2).reshape(rows, 2 * WIDTH)
    return jnp.concatenate([project[:, :WIDTH], both], axis=1)


def exchange(value, axes):
    return lax.all_to_all(value, axes, split_axis=0, concat_axis=0, tiled=True)


def after(value, *others):
    return lax.optimization_barrier((value,) + others)[0]


def per_device(
    points, cotangent, valid_counts, zorder_targets, hilbert_sources,
    zorder_project, zorder_output, hilbert_project, hilbert_output,
):
    rows = points[0]
    cot = cotangent[0]
    member = lax.axis_index(GROUP).astype(jnp.int32)
    patch = lax.axis_index(ACROSS).astype(jnp.int32)
    scal = jnp.concatenate([jnp.stack([member, patch]), valid_counts[0]])
    targets = zorder_targets[0]
    sources = hilbert_sources[0]

    meta = jnp.concatenate([sources // ROWS, sources % ROWS]).astype(BF16)
    meta = jnp.pad(meta[None], ((0, META - 1), (0, WIDTH - 2 * ROWS)))
    mine = jnp.concatenate([rows, meta], axis=0)
    near = [mine] + [
        lax.ppermute(mine, "zl", [(i, i ^ k) for i in range(4)]) for k in (1, 2, 3)
    ]

    project_z = head_pairs(zorder_project)
    project_h = head_pairs(hilbert_project)
    shard = project_z.shape[0]
    columns = jnp.concatenate(
        [
            project_z[:, WIDTH:].reshape(shard, MEMBERS, 2 * PAIR),
            project_z[:, :WIDTH].reshape(shard, MEMBERS, PAIR),
            jnp.zeros((shard, MEMBERS, PAIR), BF16),
        ],
        axis=2,
    )
    columns = jnp.transpose(columns, (1, 0, 2))
    columns = jnp.broadcast_to(columns[None], (PATCHES,) + columns.shape)
    columns = columns.reshape(PATCHES * MEMBERS, shard, 4 * PAIR)
    weights_z = exchange(columns, PTS).reshape(WIDTH, 4 * PAIR)

    later = jnp.concatenate([zorder_output, hilbert_output, project_h], axis=1)
    later = lax.all_gather(later, ("zh", "zl", "core"), axis=0, tiled=True)
    later = lax.all_gather(later, "x", axis=0, tiled=True)
    output_z = later[:, :WIDTH]
    output_h = later[:, WIDTH : 2 * WIDTH]
    project_h = later[:, 2 * WIDTH :]
    project_z = lax.all_gather(project_z, PTS, axis=0, tiled=True)

    near = jnp.concatenate(near, axis=0)
    far = lax.ppermute(near, "core", [(0, 1), (1, 0)])
    qkv_z, attended, spread, mask_z, mask_h = call(
        forward_kernel,
        [
            ((PATCH, 4 * PAIR), BF16),
            ((MEMBERS, PAIR, ROWS), BF16),
            ((PATCHES * SLOTS, ROWS), BF16),
            ((PATCH, ROWS), F32),
            ((PATCH, ROWS), F32),
        ],
        [pltpu.VMEM((PAIR, PATCH), F32)],
    )(scal, near, far, weights_z)

    attended = exchange(attended, GROUP).reshape(WIDTH, ROWS)
    send, placing = call(
        mix_kernel,
        [((PATCHES * SLOTS, 2 * WIDTH), BF16), ((PATCHES * SLOTS, ROWS), BF16)],
    )(scal, targets[None, :], targets[:, None], attended, rows, cot, output_z)

    arrived = exchange(send.reshape(PATCHES, SLOTS, 2 * WIDTH), ACROSS)
    send, rows_h, grads_h = call(
        project_kernel,
        [((MEMBERS, 2 * ROWS, ROWS), BF16), ((ROWS, WIDTH), BF16), ((ROWS, WIDTH), BF16)],
    )(scal, arrived.reshape(PATCHES * SLOTS, 2 * WIDTH), spread, project_h, output_h)
    all_grads_h = lax.all_gather(grads_h, GROUP, axis=0, tiled=True)

    arrived = exchange(send, GROUP)
    sums = [
        pltpu.VMEM((PAIR, PATCH), F32),
        pltpu.VMEM((PATCH, PAIR), F32),
        pltpu.VMEM((PATCH, PAIR), F32),
    ]
    send, attended_h = call(
        backward_h_kernel,
        [((MEMBERS, 3 * PAIR, ROWS), BF16), ((PAIR, PATCH), BF16)],
        [pltpu.VMEM((PATCH, 4 * PAIR), BF16), pltpu.VMEM((PAIR, PATCH), BF16)] + sums,
    )(scal, arrived, mask_h)

    arrived = exchange(send, GROUP)
    (send,) = call(return_kernel, [((PATCHES * SLOTS, WIDTH), BF16)])(
        scal, arrived, project_h, rows_h, grads_h, spread
    )

    arrived = exchange(send.reshape(PATCHES, SLOTS, WIDTH), ACROSS)
    grad_mixed, send = call(
        regain_kernel, [((ROWS, WIDTH), BF16), ((WIDTH, ROWS), BF16)]
    )(scal, arrived.reshape(PATCHES * SLOTS, WIDTH), placing, output_z)

    arrived = exchange(send.reshape(MEMBERS, PAIR, ROWS), GROUP)
    (send,) = call(
        backward_z_kernel,
        [((MEMBERS, 3 * PAIR, ROWS), BF16)],
        [pltpu.VMEM((PAIR, PATCH), BF16)] + sums,
    )(scal, arrived, qkv_z, mask_z)

    arrived = exchange(send, GROUP)
    (out,) = call(finish_kernel, [((ROWS, WIDTH), BF16)])(
        scal, arrived, project_z, rows, grad_mixed
    )

    factor = (lax.axis_size("scene") * PATCHES * PATCH) ** (-0.5)
    term = dot(attended_h, all_grads_h) * factor
    term = lax.psum_scatter(term, "x", scatter_dimension=0, tiled=True)
    term = lax.psum_scatter(term, "zh", scatter_dimension=0, tiled=True)
    term = lax.ppermute(
        term, PTS, [(r * MEMBERS + j, j * PATCHES + r) for r in range(PATCHES) for j in range(MEMBERS)]
    )
    term = lax.psum(term, "scene")
    return out[None], term


def solution(mesh):
    devices = mesh.devices.reshape(4, 4, 4, 2, 4)
    fine = Mesh(devices, ("x", "zh", "zl", "core", "scene"))
    rows = P("scene", PTS, None)
    index = P("scene", PTS)
    weight = P(PTS, None)
    return jax.shard_map(
        per_device,
        mesh=fine,
        in_specs=(rows, rows, P("scene", None), index, index, weight, weight, weight, weight),
        out_specs=(rows, weight),
        check_vma=False,
    )
```

```python
import functools

import jax
import jax.numpy as jnp
from jax import lax
from jax.experimental import pallas as pl
from jax.experimental.pallas import tpu as pltpu
from jax.sharding import Mesh, PartitionSpec as P

HEADS = 16
PATCH = 1024
WIDTH = 512
HEAD = 32
ROWS = 128
PAIR = 64
MEMBERS = 8
PATCHES = 16
SLOTS = 16
META = 16
SHARE = 4
SCENES = 4
EPSILON = 1e-05
NEGATIVE = -1e30
SCALE = HEAD ** (-0.5)
LOG2E = 1.4426950408889634
QBLOCK = 256

F32 = jnp.float32
BF16 = jnp.bfloat16
PTS = ("x", "zh", "zl", "core")
GROUP = ("zl", "core")
ACROSS = ("x", "zh")


def dot(a, b, ca=1, cb=0):
    return lax.dot_general(a, b, (((ca,), (cb,)), ((), ())), preferred_element_type=F32)


def normalize(values):
    center = values - jnp.mean(values, axis=1, keepdims=True)
    inverse = lax.rsqrt(jnp.mean(center * center, axis=1, keepdims=True) + EPSILON)
    return center * inverse, inverse


def normalize_back(grad, unit, inverse):
    middle = grad - jnp.mean(grad, axis=1, keepdims=True)
    return inverse * (middle - unit * jnp.mean(grad * unit, axis=1, keepdims=True))


def iota(shape, dim):
    return lax.broadcasted_iota(jnp.int32, shape, dim)


def call(kernel, outs, scratch=(), smem=1, count=1):
    def run(*args):
        specs = [pl.BlockSpec(memory_space=pltpu.SMEM)] * smem
        specs += [pl.BlockSpec(memory_space=pltpu.VMEM)] * (len(args) - smem)
        return pl.pallas_call(
            kernel,
            out_shape=[jax.ShapeDtypeStruct(s, d) for s, d in outs],
            in_specs=specs,
            out_specs=[pl.BlockSpec(memory_space=pltpu.VMEM)] * len(outs),
            scratch_shapes=list(scratch),
            compiler_params=pltpu.CompilerParams(vmem_limit_bytes=48 * 1024 * 1024),
        )(*args)

    return run


def softmax_keys(keys, query, mask):
    scores = dot(keys, query, 1, 1) * (SCALE * LOG2E)
    scores = jnp.where(mask, scores, NEGATIVE)
    weights = jnp.exp2(scores - jnp.max(scores, axis=0, keepdims=True))
    return weights * (1.0 / jnp.sum(weights, axis=0, keepdims=True))


def wide(mask_ref):
    mask = mask_ref[...]
    return jnp.concatenate([mask] * (QBLOCK // ROWS), axis=1) > 0.5


def forward_kernel(scal, gathered, weights, qkv, attended, spread, mask_z, mask_h, att):
    member = scal[0]
    limit = scal[2 + scal[1]]
    quarter = member // 2
    query_w = weights[:, : 4 * PAIR]
    keyval_w = weights[:, pl.ds(pl.multiple_of(4 * PAIR + quarter * 2 * PAIR, 2 * PAIR), 2 * PAIR)]
    stride = ROWS + META
    device = iota((ROWS, ROWS), 0)
    total = jnp.zeros((ROWS, ROWS), F32)
    flagged = jnp.zeros((ROWS, ROWS), F32)
    bound = jnp.concatenate(
        [scal[2 + k] - ROWS * iota((MEMBERS, ROWS), 0) for k in range(PATCHES)], axis=0
    ).astype(F32)
    device_f = device.astype(F32)
    for b in range(MEMBERS):
        first = b * stride
        block = gathered[first : first + ROWS, :]
        unit, _ = normalize(block.astype(F32))
        unit = unit.astype(BF16)
        rows = slice(b * ROWS, (b + 1) * ROWS)
        qkv[rows, : 2 * PAIR] = dot(unit, keyval_w).astype(BF16)
        queries = dot(unit, query_w)
        query = queries[:, :PAIR]
        for k in range(1, 4):
            query = jnp.where(quarter == k, queries[:, k * PAIR : (k + 1) * PAIR], query)
        qkv[rows, 2 * PAIR : 3 * PAIR] = query.astype(BF16)
        index = iota((ROWS, ROWS), 0) + ROWS * b
        mask_z[b * ROWS : (b + 1) * ROWS, :] = jnp.where(index < limit, 1.0, 0.0)
        meta = gathered[first + ROWS : first + stride, :].astype(F32)
        owner = meta[0:1, 0:ROWS]
        place = meta[0:1, ROWS : 2 * ROWS]
        hit = device_f == owner
        total += jnp.where(hit, 1.0, 0.0)
        flagged += jnp.where(hit & (place < bound), 1.0, 0.0)
    total = jnp.sum(total, axis=1, keepdims=True)
    flagged = jnp.sum(flagged, axis=1, keepdims=True)
    lane = iota((MEMBERS, ROWS), 1).astype(F32)
    mine = iota((MEMBERS, 1), 0) == member
    slot = iota((SLOTS, ROWS), 0).astype(F32)
    lane_slot = iota((SLOTS, ROWS), 1).astype(F32)
    offset = jnp.zeros((MEMBERS, 1), F32)
    flags = jnp.zeros((MEMBERS, ROWS), F32)
    for k in range(PATCHES):
        here = total[k * MEMBERS : (k + 1) * MEMBERS, :]
        good = flagged[k * MEMBERS : (k + 1) * MEMBERS, :]
        flags += jnp.where((lane >= offset) & (lane < offset + good), 1.0, 0.0)
        own_first = jnp.sum(jnp.where(mine, offset, 0.0), axis=0, keepdims=True)
        own_count = jnp.sum(jnp.where(mine, here, 0.0), axis=0, keepdims=True)
        spread[k * SLOTS : (k + 1) * SLOTS, :] = jnp.where(
            (slot + own_first == lane_slot) & (slot < own_count), 1.0, 0.0
        ).astype(BF16)
        offset += here
    flags = flags.astype(BF16)
    for b in range(MEMBERS):
        pick = jnp.where(iota((MEMBERS, ROWS), 0) == b, 1.0, 0.0).astype(BF16)
        mask_h[b * ROWS : (b + 1) * ROWS, :] = dot(flags, pick, 0, 0)
    mask = wide(mask_z)
    for h in range(2):
        keys = qkv[:, h * HEAD : (h + 1) * HEAD]
        values_t = qkv[:, PAIR + h * HEAD : PAIR + (h + 1) * HEAD].astype(F32).T.astype(BF16)
        for n in range(PATCH // QBLOCK):
            span = slice(n * QBLOCK, (n + 1) * QBLOCK)
            query = qkv[span, 2 * PAIR + h * HEAD : 2 * PAIR + (h + 1) * HEAD]
            probs = softmax_keys(keys, query, mask)
            att[h * HEAD : (h + 1) * HEAD, span] = dot(values_t, probs.astype(BF16))
    for b in range(MEMBERS):
        attended[b] = att[:, b * ROWS : (b + 1) * ROWS].astype(BF16)


def halves(blocks, first, last):
    return [
        jnp.concatenate([blocks[2 * x + c, :, first:last] for x in range(4)], axis=0)
        for c in range(2)
    ]


def mix_kernel(scal, targets_row, targets_col, attended, points, cotangent, output, send, placing):
    patch_row = targets_row[...] // PATCH
    patch_col = targets_col[...] // PATCH
    same = (patch_col == patch_row) & (iota((ROWS, ROWS), 0) < iota((ROWS, ROWS), 1))
    rank = jnp.sum(jnp.where(same, 1.0, 0.0), axis=0, keepdims=True).astype(jnp.int32)
    code = patch_row * SLOTS + rank
    place = jnp.where(iota((PATCHES * SLOTS, ROWS), 0) == code, 1.0, 0.0).astype(BF16)
    placing[...] = place
    weights = halves(output, 0, WIDTH // 2)
    mixed = jnp.concatenate([dot(attended[...], w, 0, 0) for w in weights], axis=1)
    mixed = points[...].astype(F32) + mixed
    send[:, :WIDTH] = dot(place, mixed.astype(BF16)).astype(BF16)
    send[:, WIDTH:] = dot(place, cotangent[...]).astype(BF16)


def project_kernel(scal, arrived, spread, project, output, send, rows, grads):
    gathered = dot(spread[...], arrived[...], 0, 0).astype(BF16)
    mixed = gathered[:, :WIDTH]
    grad = gathered[:, WIDTH:]
    rows[...] = mixed
    grads[...] = grad
    unit, _ = normalize(mixed.astype(F32))
    unit = unit.astype(BF16)
    projected = [dot(unit, w) for w in halves(project, 0, 3 * WIDTH // 2)]
    low, high = halves(output, WIDTH // 2, WIDTH)
    grad_attended = dot(grad[:, : WIDTH // 2], low, 1, 1) + dot(grad[:, WIDTH // 2 :], high, 1, 1)
    for k in range(MEMBERS):
        half, t = projected[k % 2], k // 2
        first = WIDTH // 2 + t * 2 * PAIR
        send[k, :ROWS, :] = half[:, first : first + 2 * PAIR].astype(BF16)
        send[k, ROWS:, :] = jnp.concatenate(
            [half[:, t * PAIR : (t + 1) * PAIR], grad_attended[:, k * PAIR : (k + 1) * PAIR]],
            axis=1,
        ).astype(BF16)


def backward_body(qkv, grad_t, mask, send, attended, dq, dk, dv):
    for h in range(2):
        low, high = h * HEAD, (h + 1) * HEAD
        keys = qkv[:, low:high]
        values = qkv[:, PAIR + low : PAIR + high]
        keys_t = keys.astype(F32).T.astype(BF16)
        values_t = values.astype(F32).T.astype(BF16)
        for n in range(PATCH // QBLOCK):
            span = slice(n * QBLOCK, (n + 1) * QBLOCK)
            query = qkv[span, 2 * PAIR + low : 2 * PAIR + high]
            grad = grad_t[low:high, span]
            probs = softmax_keys(keys, query, mask)
            probs_low = probs.astype(BF16)
            grad_probs = dot(values, grad)
            row_dot = jnp.sum(probs * grad_probs, axis=0, keepdims=True)
            grad_scores = (probs * (grad_probs - row_dot)).astype(BF16)
            dq[low:high, span] = dot(keys_t, grad_scores)
            part_k = dot(grad_scores, query)
            part_v = dot(probs_low, grad, 1, 1)
            if n == 0:
                dk[:, low:high] = part_k
                dv[:, low:high] = part_v
            else:
                dk[:, low:high] += part_k
                dv[:, low:high] += part_v
            if attended is not None:
                attended[low:high, span] = dot(values_t, probs_low).astype(BF16)
    for b in range(MEMBERS):
        rows = slice(b * ROWS, (b + 1) * ROWS)
        send[b, :ROWS, :] = jnp.concatenate([dk[rows, :] * SCALE, dv[rows, :]], axis=1).astype(BF16)
        send[b, ROWS:, :] = (dq[:, rows] * SCALE).astype(BF16)


def backward_h_kernel(scal, arrived, mask_h, send, attended, qkv, grad_t, dq, dk, dv):
    for b in range(MEMBERS):
        rows = slice(b * ROWS, (b + 1) * ROWS)
        qkv[rows, :ROWS] = arrived[b, :ROWS, :]
        both = arrived[b, ROWS:, :]
        qkv[rows, ROWS:] = both
        grad_t[:, rows] = both.astype(F32).T[PAIR:, :].astype(BF16)
    backward_body(qkv, grad_t, wide(mask_h), send, attended, dq, dk, dv)


def backward_z_kernel(scal, arrived, qkv, mask_z, send, grad_t, dq, dk, dv):
    for b in range(MEMBERS):
        grad_t[:, b * ROWS : (b + 1) * ROWS] = arrived[b]
    backward_body(qkv, grad_t, wide(mask_z), send, None, dq, dk, dv)


def input_grad(arrived, weights, swap, rows, grads):
    sides = []
    for c in range(2):
        members = range(c, MEMBERS, 2)
        query_part = jnp.concatenate([arrived[k, ROWS:, :].astype(F32) for k in members], axis=0)
        sides.append(
            jnp.concatenate(
                [query_part.T.astype(BF16)] + [arrived[k, :ROWS, :] for k in members], axis=1
            )
        )
    if swap is not None:
        first, second = sides
        sides = [jnp.where(swap, second, first), jnp.where(swap, first, second)]
    grad_normed = dot(sides[0], weights[0], 1, 1) + dot(sides[1], weights[1], 1, 1)
    unit, inverse = normalize(rows[...].astype(F32))
    return (grads[...].astype(F32) + normalize_back(grad_normed, unit, inverse)).astype(BF16)


def return_kernel(scal, arrived, project, rows, grads, spread, attended, all_grads, send):
    grad = input_grad(arrived, halves(project, 0, 3 * WIDTH // 2), None, rows, grads)
    spaced = dot(spread[...], grad).astype(BF16)
    term = dot(attended[...], all_grads[...])
    upper = term.astype(BF16)
    lower = (term - upper.astype(F32)).astype(BF16)
    for k in range(PATCHES):
        send[k, :SLOTS, :] = spaced[k * SLOTS : (k + 1) * SLOTS, :]
        share = slice(k * SHARE, (k + 1) * SHARE)
        send[k, SLOTS:, :] = jnp.concatenate([upper[share, :], lower[share, :]], axis=0)


def regain_kernel(scal, arrived, placing, output, grad_mixed, send, term):
    spaced = jnp.concatenate([arrived[k, :SLOTS, :] for k in range(PATCHES)], axis=0)
    grad = dot(placing[...], spaced, 0, 0).astype(BF16)
    grad_mixed[...] = grad
    low, high = halves(output, 0, WIDTH // 2)
    grad_attended = dot(low, grad[:, : WIDTH // 2], 1, 1) + dot(high, grad[:, WIDTH // 2 :], 1, 1)
    send[...] = grad_attended.astype(BF16)
    total = jnp.zeros((2 * SHARE, WIDTH), F32)
    for k in range(PATCHES):
        total += arrived[k, SLOTS:, :].astype(F32)
    factor = (SCENES * PATCHES * PATCH) ** (-0.5)
    term[...] = (total[:SHARE, :] + total[SHARE:, :]) * factor


def finish_kernel(scal, arrived, project, other, rows, grads, out):
    weights = [project[...], other[...]]
    out[...] = input_grad(arrived, weights, scal[0] % 2 == 1, rows, grads)


def by_core(project):
    shard = project.shape[0]
    pairs = jnp.transpose(project.reshape(shard, 3, 4, 2, PAIR), (3, 0, 1, 2, 4))
    queries = pairs[:, :, 0].reshape(2, shard, 4 * PAIR)
    both = jnp.stack([pairs[:, :, 1], pairs[:, :, 2]], axis=3).reshape(2, shard, 8 * PAIR)
    return jnp.concatenate([queries, both], axis=2)


def by_half(output):
    return jnp.transpose(output.reshape(output.shape[0], 2, WIDTH // 2), (1, 0, 2))


def exchange(value, axes):
    return lax.all_to_all(value, axes, split_axis=0, concat_axis=0, tiled=True)


def per_device(
    points, cotangent, valid_counts, zorder_targets, hilbert_sources,
    zorder_project, zorder_output, hilbert_project, hilbert_output,
):
    rows = points[0]
    cot = cotangent[0]
    member = lax.axis_index(GROUP).astype(jnp.int32)
    patch = lax.axis_index(ACROSS).astype(jnp.int32)
    scal = jnp.concatenate([jnp.stack([member, patch]), valid_counts[0]])
    targets = zorder_targets[0]
    sources = hilbert_sources[0]

    meta = jnp.concatenate([sources // ROWS, sources % ROWS]).astype(BF16)
    meta = jnp.pad(meta[None], ((0, META - 1), (0, WIDTH - 2 * ROWS)))
    gathered = lax.all_gather(jnp.concatenate([rows, meta], axis=0), GROUP, axis=0, tiled=True)

    weights = jnp.concatenate(
        [by_core(zorder_project), by_core(hilbert_project), by_half(zorder_output), by_half(hilbert_output)],
        axis=2,
    )
    weights = exchange(weights, "core").reshape(MEMBERS, 4 * WIDTH)
    weights = lax.all_gather(weights, ("zh", "zl"), axis=0, tiled=True)
    third = 3 * WIDTH // 2
    project_z = lax.all_gather(weights[:, :third], "x", axis=0, tiled=True)
    outputs = lax.all_gather(weights[:, 2 * third :], ("x", "core"), axis=0, tiled=True)
    outputs = outputs.reshape(MEMBERS, ROWS, WIDTH)
    project_h = lax.all_gather(weights[:, third : 2 * third], ("x", "core"), axis=0, tiled=True)
    project_h = project_h.reshape(MEMBERS, ROWS, third)
    other_z = lax.ppermute(project_z, "core", [(0, 1), (1, 0)])

    qkv_z, attended, spread, mask_z, mask_h = call(
        forward_kernel,
        [
            ((PATCH, 4 * PAIR), BF16),
            ((MEMBERS, PAIR, ROWS), BF16),
            ((PATCHES * SLOTS, ROWS), BF16),
            ((PATCH, ROWS), F32),
            ((PATCH, ROWS), F32),
        ],
        [pltpu.VMEM((PAIR, PATCH), F32)],
    )(scal, gathered, project_z)

    attended = exchange(attended, GROUP).reshape(WIDTH, ROWS)
    send, placing = call(
        mix_kernel,
        [((PATCHES * SLOTS, 2 * WIDTH), BF16), ((PATCHES * SLOTS, ROWS), BF16)],
    )(scal, targets[None, :], targets[:, None], attended, rows, cot, outputs)

    arrived = exchange(send.reshape(PATCHES, SLOTS, 2 * WIDTH), ACROSS)
    send, rows_h, grads_h = call(
        project_kernel,
        [((MEMBERS, 2 * ROWS, ROWS), BF16), ((ROWS, WIDTH), BF16), ((ROWS, WIDTH), BF16)],
    )(scal, arrived.reshape(PATCHES * SLOTS, 2 * WIDTH), spread, project_h, outputs)
    all_grads_h = lax.all_gather(grads_h, GROUP, axis=0, tiled=True)

    arrived = exchange(send, GROUP)
    sums = [
        pltpu.VMEM((PAIR, PATCH), F32),
        pltpu.VMEM((PATCH, PAIR), F32),
        pltpu.VMEM((PATCH, PAIR), F32),
    ]
    send, attended_h = call(
        backward_h_kernel,
        [((MEMBERS, 3 * PAIR, ROWS), BF16), ((PAIR, PATCH), BF16)],
        [pltpu.VMEM((PATCH, 4 * PAIR), BF16), pltpu.VMEM((PAIR, PATCH), BF16)] + sums,
    )(scal, arrived, mask_h)

    arrived = exchange(send, GROUP)
    (send,) = call(return_kernel, [((PATCHES, SLOTS + 2 * SHARE, WIDTH), BF16)])(
        scal, arrived, project_h, rows_h, grads_h, spread, attended_h, all_grads_h
    )

    arrived = exchange(send, ACROSS)
    grad_mixed, send, term = call(
        regain_kernel,
        [((ROWS, WIDTH), BF16), ((WIDTH, ROWS), BF16), ((SHARE, WIDTH), F32)],
    )(scal, arrived, placing, outputs)
    beside = lax.ppermute(term, "scene", [(i, i ^ 1) for i in range(SCENES)])
    arrived = exchange(send.reshape(MEMBERS, PAIR, ROWS), GROUP)
    arrived, beside = lax.optimization_barrier((arrived, beside))
    term = term + beside
    moves = [(r * MEMBERS + j, j * PATCHES + r) for r in range(PATCHES) for j in range(MEMBERS)]
    moved = lax.ppermute(term, PTS, moves)
    crossed = lax.ppermute(
        term,
        PTS + ("scene",),
        [(a * SCENES + i, b * SCENES + (i ^ 2)) for a, b in moves for i in range(SCENES)],
    )

    (send,) = call(
        backward_z_kernel,
        [((MEMBERS, 3 * PAIR, ROWS), BF16)],
        [pltpu.VMEM((PAIR, PATCH), BF16)] + sums,
    )(scal, arrived, qkv_z, mask_z)
    send, moved, crossed = lax.optimization_barrier((send, moved, crossed))

    arrived = exchange(send, GROUP)
    (out,) = call(finish_kernel, [((ROWS, WIDTH), BF16)])(
        scal, arrived, project_z, other_z, rows, grad_mixed
    )

    return out[None], moved + crossed


def solution(mesh):
    devices = mesh.devices.reshape(4, 4, 4, 2, 4)
    fine = Mesh(devices, ("x", "zh", "zl", "core", "scene"))
    rows = P("scene", PTS, None)
    index = P("scene", PTS)
    weight = P(PTS, None)
    return jax.shard_map(
        per_device,
        mesh=fine,
        in_specs=(rows, rows, P("scene", None), index, index, weight, weight, weight, weight),
        out_specs=(rows, weight),
        check_vma=False,
    )
```

```python
import functools

import jax
import jax.numpy as jnp
from jax import lax
from jax.experimental import pallas as pl
from jax.experimental.pallas import tpu as pltpu
from jax.sharding import Mesh, PartitionSpec as P

HEADS = 16
PATCH = 1024
WIDTH = 512
HEAD = 32
ROWS = 128
PAIR = 64
MEMBERS = 8
PATCHES = 16
SLOTS = 16
META = 16
SHARE = 4
SCENES = 4
PROJECT_H = (0, 768)
OUTPUT_Z = (768, 1024)
OUTPUT_H = (1024, 1280)
EPSILON = 1e-05
NEGATIVE = -1e30
SCALE = HEAD ** (-0.5)
LOG2E = 1.4426950408889634
QBLOCK = 256

F32 = jnp.float32
BF16 = jnp.bfloat16
PTS = ("x", "zh", "zl", "core")
GROUP = ("zl", "core")
ACROSS = ("x", "zh")


def dot(a, b, ca=1, cb=0):
    return lax.dot_general(a, b, (((ca,), (cb,)), ((), ())), preferred_element_type=F32)


def normalize(values):
    center = values - jnp.mean(values, axis=1, keepdims=True)
    inverse = lax.rsqrt(jnp.mean(center * center, axis=1, keepdims=True) + EPSILON)
    return center * inverse, inverse


def normalize_back(grad, unit, inverse):
    middle = grad - jnp.mean(grad, axis=1, keepdims=True)
    return inverse * (middle - unit * jnp.mean(grad * unit, axis=1, keepdims=True))


def iota(shape, dim):
    return lax.broadcasted_iota(jnp.int32, shape, dim)


def call(kernel, ins, outs, scratch=(), limit=32):
    views = [item[1:] if isinstance(item, tuple) else None for item in ins]
    arrays = [item[0] if isinstance(item, tuple) else item for item in ins]
    scalars = [a.ndim == 1 for a in arrays]

    def body(*refs):
        given = list(refs)
        for k, view in enumerate(views):
            if view is not None:
                lead = (slice(None),) * (len(arrays[k].shape) - 1)
                given[k] = refs[k].at[lead + (pl.ds(view[0], view[1] - view[0]),)]
        kernel(*given)

    return pl.pallas_call(
        body,
        out_shape=[jax.ShapeDtypeStruct(shape, dtype) for shape, dtype in outs],
        in_specs=[pl.BlockSpec(memory_space=pltpu.SMEM if flat else pltpu.VMEM) for flat in scalars],
        out_specs=[pl.BlockSpec(memory_space=pltpu.VMEM) for _ in outs],
        scratch_shapes=list(scratch),
        compiler_params=pltpu.CompilerParams(vmem_limit_bytes=limit * 1024 * 1024),
    )(*arrays)


def softmax_keys(keys, query, mask):
    scores = dot(keys, query, 1, 1) * (SCALE * LOG2E)
    scores = jnp.where(mask, scores, NEGATIVE)
    weights = jnp.exp2(scores - jnp.max(scores, axis=0, keepdims=True))
    return weights * (1.0 / jnp.sum(weights, axis=0, keepdims=True))


def key_mask(flags):
    parts = []
    for b in range(MEMBERS):
        pick = jnp.where(iota((MEMBERS, QBLOCK), 0) == b, 1.0, 0.0).astype(BF16)
        parts.append(dot(flags, pick, 0, 0))
    return jnp.concatenate(parts, axis=0) > 0.5


def place_rows(targets):
    patch = targets[...] // PATCH
    patches = jnp.broadcast_to(patch, (MEMBERS, ROWS)).astype(F32)
    column = jnp.broadcast_to(patches.T[:, :1], (ROWS, ROWS))
    row = jnp.broadcast_to(patch, (ROWS, ROWS)).astype(F32)
    same = (column == row) & (iota((ROWS, ROWS), 0) < iota((ROWS, ROWS), 1))
    rank = jnp.sum(jnp.where(same, 1.0, 0.0), axis=0, keepdims=True).astype(jnp.int32)
    code = patch * SLOTS + rank
    return jnp.where(iota((PATCHES * SLOTS, ROWS), 0) == code, 1.0, 0.0).astype(BF16)


def prepare_kernel(points, sources, project_z, project_h, output_z, output_h, mine, weights):
    mine[:ROWS, :] = points[...]
    source = sources[...]
    digits = jnp.concatenate([source // ROWS, source % ROWS], axis=1).astype(F32)
    digits = jnp.concatenate([digits, jnp.zeros((1, WIDTH - 2 * ROWS), F32)], axis=1)
    mine[ROWS:, :] = jnp.broadcast_to(digits, (META, WIDTH)).astype(BF16)
    for c in range(2):
        pieces = []
        for project in (project_z, project_h):
            values = project[...].astype(F32)
            pairs = range(c, MEMBERS, 2)
            pieces += [values[:, k * PAIR : (k + 1) * PAIR] for k in pairs]
            for k in pairs:
                pieces += [
                    values[:, n * WIDTH + k * PAIR : n * WIDTH + (k + 1) * PAIR] for n in (1, 2)
                ]
        for output in (output_z, output_h):
            half = WIDTH // 2
            pieces.append(output[:, c * half : (c + 1) * half].astype(F32))
        weights[c] = jnp.concatenate(pieces, axis=1).astype(BF16)


def forward_kernel(scal, gathered, weights, qkv, attended, plan, att):
    member = scal[0]
    limit = scal[2 + scal[1]]
    w = weights[...]
    stride = ROWS + META
    source = gathered
    device = iota((ROWS, ROWS), 0)
    total = jnp.zeros((ROWS, ROWS), F32)
    flagged = jnp.zeros((ROWS, ROWS), F32)
    bound = jnp.concatenate(
        [scal[2 + k] - ROWS * iota((MEMBERS, ROWS), 0) for k in range(PATCHES)], axis=0
    ).astype(F32)
    device_f = device.astype(F32)
    for b in range(MEMBERS):
        first = b * stride
        block = source[first : first + ROWS, :]
        unit, _ = normalize(block.astype(F32))
        unit = unit.astype(BF16)
        rows = slice(b * ROWS, (b + 1) * ROWS)
        qkv[rows, :] = dot(unit, w).astype(BF16)
        meta = source[first + ROWS : first + stride, :].astype(F32)
        owner = meta[0:1, 0:ROWS]
        place = meta[0:1, ROWS : 2 * ROWS]
        hit = device_f == owner
        total += jnp.where(hit, 1.0, 0.0)
        flagged += jnp.where(hit & (place < bound), 1.0, 0.0)
    total = jnp.sum(total, axis=1, keepdims=True)
    flagged = jnp.sum(flagged, axis=1, keepdims=True)
    lane = iota((MEMBERS, ROWS), 1).astype(F32)
    mine = iota((MEMBERS, 1), 0) == member
    slot = iota((SLOTS, ROWS), 0).astype(F32)
    lane_slot = iota((SLOTS, ROWS), 1).astype(F32)
    offset = jnp.zeros((MEMBERS, 1), F32)
    flags = jnp.zeros((MEMBERS, ROWS), F32)
    for k in range(PATCHES):
        here = total[k * MEMBERS : (k + 1) * MEMBERS, :]
        good = flagged[k * MEMBERS : (k + 1) * MEMBERS, :]
        flags += jnp.where((lane >= offset) & (lane < offset + good), 1.0, 0.0)
        own_first = jnp.sum(jnp.where(mine, offset, 0.0), axis=0, keepdims=True)
        own_count = jnp.sum(jnp.where(mine, here, 0.0), axis=0, keepdims=True)
        plan[k * SLOTS : (k + 1) * SLOTS, :] = jnp.where(
            (slot + own_first == lane_slot) & (slot < own_count), 1.0, 0.0
        ).astype(BF16)
        offset += here
    plan[PATCHES * SLOTS :, :] = jnp.concatenate([flags, flags], axis=0).astype(BF16)
    mask = iota((PATCH, QBLOCK), 0) < limit
    for h in range(2):
        keys = qkv[:, h * HEAD : (h + 1) * HEAD]
        values_t = qkv[:, PAIR + h * HEAD : PAIR + (h + 1) * HEAD].astype(F32).T.astype(BF16)
        for n in range(PATCH // QBLOCK):
            span = slice(n * QBLOCK, (n + 1) * QBLOCK)
            query = qkv[span, 2 * PAIR + h * HEAD : 2 * PAIR + (h + 1) * HEAD]
            probs = softmax_keys(keys, query, mask)
            att[h * HEAD : (h + 1) * HEAD, span] = dot(values_t, probs.astype(BF16))
    for b in range(MEMBERS):
        attended[b] = att[:, b * ROWS : (b + 1) * ROWS].astype(BF16)


def halves(blocks, first, last):
    return [
        jnp.concatenate([blocks[2 * x + c, :, first:last] for x in range(4)], axis=0)
        for c in range(2)
    ]


def mix_kernel(targets, attended, points, cotangent, shared, send):
    place = place_rows(targets)
    weights = halves(shared, 0, WIDTH // 2)
    mixed = jnp.concatenate([dot(attended[...], w, 0, 0) for w in weights], axis=1)
    mixed = points[...].astype(F32) + mixed
    send[:, :WIDTH] = dot(place, mixed.astype(BF16)).astype(BF16)
    send[:, WIDTH:] = dot(place, cotangent[...]).astype(BF16)


def project_kernel(arrived, plan, project, output, send, rows_out, grads_out):
    gathered = dot(plan[: PATCHES * SLOTS, :], arrived[...], 0, 0).astype(BF16)
    mixed = gathered[:, :WIDTH]
    grad = gathered[:, WIDTH:]
    grads_out[...] = grad
    rows_out[...] = mixed
    unit, _ = normalize(mixed.astype(F32))
    unit = unit.astype(BF16)
    projected = [dot(unit, w) for w in halves(project, 0, 3 * WIDTH // 2)]
    low, high = halves(output, 0, WIDTH // 2)
    grad_attended = dot(grad[:, : WIDTH // 2], low, 1, 1) + dot(grad[:, WIDTH // 2 :], high, 1, 1)
    for k in range(MEMBERS):
        half, t = projected[k % 2], k // 2
        first = WIDTH // 2 + t * 2 * PAIR
        send[k, :ROWS, :] = half[:, first : first + 2 * PAIR].astype(BF16)
        send[k, ROWS:, :] = jnp.concatenate(
            [half[:, t * PAIR : (t + 1) * PAIR], grad_attended[:, k * PAIR : (k + 1) * PAIR]],
            axis=1,
        ).astype(BF16)


def backward_body(qkv, grad_t, mask, send, attended, dq, dk, dv):
    for h in range(2):
        low, high = h * HEAD, (h + 1) * HEAD
        keys = qkv[:, low:high]
        values = qkv[:, PAIR + low : PAIR + high]
        keys_t = keys.astype(F32).T.astype(BF16)
        values_t = values.astype(F32).T.astype(BF16)
        for n in range(PATCH // QBLOCK):
            span = slice(n * QBLOCK, (n + 1) * QBLOCK)
            query = qkv[span, 2 * PAIR + low : 2 * PAIR + high]
            grad = grad_t[low:high, span]
            probs = softmax_keys(keys, query, mask)
            probs_low = probs.astype(BF16)
            grad_probs = dot(values, grad)
            row_dot = jnp.sum(probs * grad_probs, axis=0, keepdims=True)
            grad_scores = (probs * (grad_probs - row_dot)).astype(BF16)
            dq[low:high, span] = dot(keys_t, grad_scores)
            part_k = dot(grad_scores, query)
            part_v = dot(probs_low, grad, 1, 1)
            if n == 0:
                dk[:, low:high] = part_k
                dv[:, low:high] = part_v
            else:
                dk[:, low:high] += part_k
                dv[:, low:high] += part_v
            if attended is not None:
                attended[low:high, span] = dot(values_t, probs_low).astype(BF16)
    for b in range(MEMBERS):
        rows = slice(b * ROWS, (b + 1) * ROWS)
        send[b, :ROWS, :] = jnp.concatenate([dk[rows, :] * SCALE, dv[rows, :]], axis=1).astype(BF16)
        send[b, ROWS:, :] = (dq[:, rows] * SCALE).astype(BF16)


def backward_h_kernel(arrived, plan, send, attended, qkv, grad_t, dq, dk, dv):
    for b in range(MEMBERS):
        rows = slice(b * ROWS, (b + 1) * ROWS)
        qkv[rows, :ROWS] = arrived[b, :ROWS, :]
        both = arrived[b, ROWS:, :]
        qkv[rows, ROWS:] = both
        grad_t[:, rows] = both.astype(F32).T[PAIR:, :].astype(BF16)
    mask = key_mask(plan[PATCHES * SLOTS : PATCHES * SLOTS + MEMBERS, :])
    backward_body(qkv, grad_t, mask, send, attended, dq, dk, dv)


def backward_z_kernel(scal, arrived, qkv, send, grad_t, dq, dk, dv):
    for b in range(MEMBERS):
        grad_t[:, b * ROWS : (b + 1) * ROWS] = arrived[b]
    mask = iota((PATCH, QBLOCK), 0) < scal[2 + scal[1]]
    backward_body(qkv, grad_t, mask, send, None, dq, dk, dv)


def input_grad(arrived, weights, rows, grads):
    sides = []
    for c in range(2):
        members = range(c, MEMBERS, 2)
        query_part = jnp.concatenate([arrived[k, ROWS:, :].astype(F32) for k in members], axis=0)
        sides.append(
            jnp.concatenate(
                [query_part.T.astype(BF16)] + [arrived[k, :ROWS, :] for k in members], axis=1
            )
        )
    grad_normed = dot(sides[0], weights[0], 1, 1) + dot(sides[1], weights[1], 1, 1)
    unit, inverse = normalize(rows[...].astype(F32))
    return (grads[...].astype(F32) + normalize_back(grad_normed, unit, inverse)).astype(BF16)


def return_kernel(arrived, project, rows, grads, plan, attended, all_grads, send):
    grad = input_grad(arrived, halves(project, 0, 3 * WIDTH // 2), rows, grads)
    spaced = dot(plan[: PATCHES * SLOTS, :], grad).astype(BF16)
    term = dot(attended[...], all_grads[...])
    upper = term.astype(BF16)
    lower = (term - upper.astype(F32)).astype(BF16)
    for k in range(PATCHES):
        send[k, :SLOTS, :] = spaced[k * SLOTS : (k + 1) * SLOTS, :]
        share = slice(k * SHARE, (k + 1) * SHARE)
        send[k, SLOTS:, :] = jnp.concatenate([upper[share, :], lower[share, :]], axis=0)


def regain_kernel(arrived, targets, output, grad_mixed, send, term):
    spaced = jnp.concatenate([arrived[k, :SLOTS, :] for k in range(PATCHES)], axis=0)
    grad = dot(place_rows(targets), spaced, 0, 0).astype(BF16)
    grad_mixed[...] = grad
    low, high = halves(output, 0, WIDTH // 2)
    grad_attended = dot(low, grad[:, : WIDTH // 2], 1, 1) + dot(high, grad[:, WIDTH // 2 :], 1, 1)
    send[...] = grad_attended.astype(BF16)
    total = jnp.zeros((2 * SHARE, WIDTH), F32)
    for k in range(PATCHES):
        total += arrived[k, SLOTS:, :].astype(F32)
    factor = (SCENES * PATCHES * PATCH) ** (-0.5)
    term[...] = (total[:SHARE, :] + total[SHARE:, :]) * factor


def finish_kernel(arrived, project, rows, grads, out):
    out[...] = input_grad(arrived, halves(project, 0, 3 * WIDTH // 2), rows, grads)


def exchange(value, axes):
    return lax.all_to_all(value, axes, split_axis=0, concat_axis=0, tiled=True)


def per_device(
    points, cotangent, valid_counts, zorder_targets, hilbert_sources,
    zorder_project, zorder_output, hilbert_project, hilbert_output,
):
    rows = points[0]
    cot = cotangent[0]
    member = lax.axis_index(GROUP).astype(jnp.int32)
    patch = lax.axis_index(ACROSS).astype(jnp.int32)
    scal = jnp.concatenate([jnp.stack([member, patch]), valid_counts[0]])
    targets = zorder_targets[0]
    sources = hilbert_sources[0]

    mine, weights = call(
        prepare_kernel,
        [rows, sources[None, :], zorder_project, hilbert_project, zorder_output, hilbert_output],
        [((ROWS + META, WIDTH), BF16), ((2, SHARE, 4 * WIDTH), BF16)],
    )
    gathered = lax.all_gather(mine, GROUP, axis=0, tiled=True)
    weights = exchange(weights, "core").reshape(MEMBERS, 4 * WIDTH)
    weights = lax.all_gather(weights, ("zh", "zl"), axis=0, tiled=True)
    third = 3 * WIDTH // 2
    quarter = lax.axis_index("zl")
    own = jnp.concatenate(
        [
            lax.dynamic_slice_in_dim(weights, 4 * PAIR + quarter * 2 * PAIR, 2 * PAIR, 1),
            lax.dynamic_slice_in_dim(weights, quarter * PAIR, PAIR, 1),
            jnp.zeros((ROWS, PAIR), BF16),
        ],
        axis=1,
    )
    own = lax.all_gather(own, "x", axis=0, tiled=True)
    shared = lax.all_gather(weights[:, third:], ("x", "core"), axis=0, tiled=True)
    shared = shared.reshape(MEMBERS, ROWS, third + WIDTH)
    project_z = lax.all_gather(weights[:, :third], ("x", "core"), axis=0, tiled=True)
    project_z = project_z.reshape(MEMBERS, ROWS, third)

    targets = targets[None, :]
    qkv_z, attended, plan = call(
        forward_kernel,
        [scal, gathered, own],
        [
            ((PATCH, 4 * PAIR), BF16),
            ((MEMBERS, PAIR, ROWS), BF16),
            ((PATCHES * SLOTS + 2 * MEMBERS, ROWS), BF16),
        ],
        [pltpu.VMEM((PAIR, PATCH), F32)],
    )

    attended = exchange(attended, GROUP).reshape(WIDTH, ROWS)
    (send,) = call(
        mix_kernel,
        [targets, attended, rows, cot, (shared, *OUTPUT_Z)],
        [((PATCHES * SLOTS, 2 * WIDTH), BF16)],
    )

    arrived = exchange(send.reshape(PATCHES, SLOTS, 2 * WIDTH), ACROSS)
    send, rows_h, grads_h = call(
        project_kernel,
        [
            arrived.reshape(PATCHES * SLOTS, 2 * WIDTH),
            plan,
            (shared, *PROJECT_H),
            (shared, *OUTPUT_H),
        ],
        [((MEMBERS, 2 * ROWS, ROWS), BF16), ((ROWS, WIDTH), BF16), ((ROWS, WIDTH), BF16)],
    )
    all_grads_h = lax.all_gather(grads_h, GROUP, axis=0, tiled=True)

    arrived = exchange(send, GROUP)
    sums = [
        pltpu.VMEM((PAIR, PATCH), F32),
        pltpu.VMEM((PATCH, PAIR), F32),
        pltpu.VMEM((PATCH, PAIR), F32),
    ]
    send, attended_h = call(
        backward_h_kernel,
        [arrived, plan],
        [((MEMBERS, 3 * PAIR, ROWS), BF16), ((PAIR, PATCH), BF16)],
        [pltpu.VMEM((PATCH, 4 * PAIR), BF16), pltpu.VMEM((PAIR, PATCH), BF16)] + sums,
    )

    arrived = exchange(send, GROUP)
    (send,) = call(
        return_kernel,
        [arrived, (shared, *PROJECT_H), rows_h, grads_h, plan, attended_h, all_grads_h],
        [((PATCHES, SLOTS + 2 * SHARE, WIDTH), BF16)],
    )

    arrived = exchange(send, ACROSS)
    grad_mixed, send, term = call(
        regain_kernel,
        [arrived, targets, (shared, *OUTPUT_Z)],
        [((ROWS, WIDTH), BF16), ((WIDTH, ROWS), BF16), ((SHARE, WIDTH), F32)],
    )
    beside = lax.ppermute(term, "scene", [(i, i ^ 1) for i in range(SCENES)])
    arrived = exchange(send.reshape(MEMBERS, PAIR, ROWS), GROUP)
    arrived, beside = lax.optimization_barrier((arrived, beside))
    term = term + beside
    beside = lax.ppermute(term, "scene", [(i, i ^ 2) for i in range(SCENES)])
    (send,) = call(
        backward_z_kernel,
        [scal, arrived, qkv_z],
        [((MEMBERS, 3 * PAIR, ROWS), BF16)],
        [pltpu.VMEM((PAIR, PATCH), BF16)] + sums,
    )
    send, term, beside = lax.optimization_barrier((send, term, beside))
    term = lax.ppermute(
        term + beside,
        PTS,
        [(r * MEMBERS + j, j * PATCHES + r) for r in range(PATCHES) for j in range(MEMBERS)],
    )

    arrived = exchange(send, GROUP)
    (out,) = call(finish_kernel, [arrived, project_z, rows, grad_mixed], [((ROWS, WIDTH), BF16)])
    return out[None], term


def solution(mesh):
    devices = mesh.devices.reshape(4, 4, 4, 2, 4)
    fine = Mesh(devices, ("x", "zh", "zl", "core", "scene"))
    rows = P("scene", PTS, None)
    index = P("scene", PTS)
    weight = P(PTS, None)
    return jax.shard_map(
        per_device,
        mesh=fine,
        in_specs=(rows, rows, P("scene", None), index, index, weight, weight, weight, weight),
        out_specs=(rows, weight),
        check_vma=False,
    )
```

```python
import functools

import jax
import jax.numpy as jnp
from jax import lax
from jax.experimental import pallas as pl
from jax.experimental.pallas import tpu as pltpu
from jax.sharding import Mesh, PartitionSpec as P

HEADS = 16
PATCH = 1024
WIDTH = 512
HEAD = 32
ROWS = 128
PAIR = 64
MEMBERS = 8
PATCHES = 16
SLOTS = 16
META = 16
SHARE = 4
SCENES = 4
PROJECT_H = (0, 768)
OUTPUT_Z = (768, 1024)
OUTPUT_H = (1024, 1280)
EPSILON = 1e-05
NEGATIVE = -1e30
SCALE = HEAD ** (-0.5)
LOG2E = 1.4426950408889634
QBLOCK = 256
MICRO = 1_150_000_000

F32 = jnp.float32
BF16 = jnp.bfloat16
PTS = ("x", "zh", "zl", "core")
GROUP = ("zl", "core")
ACROSS = ("x", "zh")


def dot(a, b, ca=1, cb=0):
    return lax.dot_general(a, b, (((ca,), (cb,)), ((), ())), preferred_element_type=F32)


def normalize(values):
    center = values - jnp.mean(values, axis=1, keepdims=True)
    inverse = lax.rsqrt(jnp.mean(center * center, axis=1, keepdims=True) + EPSILON)
    return center * inverse, inverse


def normalize_back(grad, unit, inverse):
    middle = grad - jnp.mean(grad, axis=1, keepdims=True)
    return inverse * (middle - unit * jnp.mean(grad * unit, axis=1, keepdims=True))


def iota(shape, dim):
    return lax.broadcasted_iota(jnp.int32, shape, dim)


def call(kernel, ins, outs, scratch=(), limit=32, micros=1):
    views = [item[1:] if isinstance(item, tuple) else None for item in ins]
    arrays = [item[0] if isinstance(item, tuple) else item for item in ins]
    scalars = [a.ndim == 1 for a in arrays]

    def body(*refs):
        given = list(refs)
        for k, view in enumerate(views):
            if view is not None:
                lead = (slice(None),) * (len(arrays[k].shape) - 1)
                given[k] = refs[k].at[lead + (pl.ds(view[0], view[1] - view[0]),)]
        kernel(*given)

    return pl.pallas_call(
        body,
        out_shape=[jax.ShapeDtypeStruct(shape, dtype) for shape, dtype in outs],
        in_specs=[pl.BlockSpec(memory_space=pltpu.SMEM if flat else pltpu.VMEM) for flat in scalars],
        out_specs=[pl.BlockSpec(memory_space=pltpu.VMEM) for _ in outs],
        scratch_shapes=list(scratch),
        cost_estimate=pl.CostEstimate(flops=micros * MICRO, bytes_accessed=0, transcendentals=0),
        compiler_params=pltpu.CompilerParams(vmem_limit_bytes=limit * 1024 * 1024),
    )(*arrays)


def softmax_keys(keys, query, mask):
    scores = dot(keys, query, 1, 1) * (SCALE * LOG2E)
    scores = jnp.where(mask, scores, NEGATIVE)
    weights = jnp.exp2(scores - jnp.max(scores, axis=0, keepdims=True))
    return weights * (1.0 / jnp.sum(weights, axis=0, keepdims=True))


def key_mask(flags):
    parts = []
    for b in range(MEMBERS):
        pick = jnp.where(iota((MEMBERS, QBLOCK), 0) == b, 1.0, 0.0).astype(BF16)
        parts.append(dot(flags, pick, 0, 0))
    return jnp.concatenate(parts, axis=0) > 0.5


def place_rows(targets):
    patch = targets[...] // PATCH
    patches = jnp.broadcast_to(patch, (MEMBERS, ROWS)).astype(F32)
    column = jnp.broadcast_to(patches.T[:, :1], (ROWS, ROWS))
    row = jnp.broadcast_to(patch, (ROWS, ROWS)).astype(F32)
    same = (column == row) & (iota((ROWS, ROWS), 0) < iota((ROWS, ROWS), 1))
    rank = jnp.sum(jnp.where(same, 1.0, 0.0), axis=0, keepdims=True).astype(jnp.int32)
    code = patch * SLOTS + rank
    return jnp.where(iota((PATCHES * SLOTS, ROWS), 0) == code, 1.0, 0.0).astype(BF16)


def prepare_kernel(
    points, cotangent, targets, sources, project_z, project_h, output_z, output_h, mine, weights, grads
):
    grads[...] = dot(place_rows(targets), cotangent[...]).astype(BF16)
    mine[:ROWS, :] = points[...]
    source = sources[...]
    digits = jnp.concatenate([source // ROWS, source % ROWS], axis=1).astype(F32)
    digits = jnp.concatenate([digits, jnp.zeros((1, WIDTH - 2 * ROWS), F32)], axis=1)
    mine[ROWS:, :] = jnp.broadcast_to(digits, (META, WIDTH)).astype(BF16)
    for c in range(2):
        pieces = []
        for project in (project_z, project_h):
            values = project[...].astype(F32)
            pairs = range(c, MEMBERS, 2)
            pieces += [values[:, k * PAIR : (k + 1) * PAIR] for k in pairs]
            for k in pairs:
                pieces += [
                    values[:, n * WIDTH + k * PAIR : n * WIDTH + (k + 1) * PAIR] for n in (1, 2)
                ]
        for output in (output_z, output_h):
            half = WIDTH // 2
            pieces.append(output[:, c * half : (c + 1) * half].astype(F32))
        weights[c] = jnp.concatenate(pieces, axis=1).astype(BF16)


def forward_kernel(scal, gathered, weights, qkv, attended, plan, att):
    member = scal[0]
    limit = scal[2 + scal[1]]
    w = weights[...]
    stride = ROWS + META
    source = gathered
    device = iota((ROWS, ROWS), 0)
    total = jnp.zeros((ROWS, ROWS), F32)
    flagged = jnp.zeros((ROWS, ROWS), F32)
    bound = jnp.concatenate(
        [scal[2 + k] - ROWS * iota((MEMBERS, ROWS), 0) for k in range(PATCHES)], axis=0
    ).astype(F32)
    device_f = device.astype(F32)
    for b in range(MEMBERS):
        first = b * stride
        block = source[first : first + ROWS, :]
        unit, _ = normalize(block.astype(F32))
        unit = unit.astype(BF16)
        rows = slice(b * ROWS, (b + 1) * ROWS)
        qkv[rows, :] = dot(unit, w).astype(BF16)
        meta = source[first + ROWS : first + stride, :].astype(F32)
        owner = meta[0:1, 0:ROWS]
        place = meta[0:1, ROWS : 2 * ROWS]
        hit = device_f == owner
        total += jnp.where(hit, 1.0, 0.0)
        flagged += jnp.where(hit & (place < bound), 1.0, 0.0)
    total = jnp.sum(total, axis=1, keepdims=True)
    flagged = jnp.sum(flagged, axis=1, keepdims=True)
    lane = iota((MEMBERS, ROWS), 1).astype(F32)
    mine = iota((MEMBERS, 1), 0) == member
    slot = iota((SLOTS, ROWS), 0).astype(F32)
    lane_slot = iota((SLOTS, ROWS), 1).astype(F32)
    offset = jnp.zeros((MEMBERS, 1), F32)
    flags = jnp.zeros((MEMBERS, ROWS), F32)
    for k in range(PATCHES):
        here = total[k * MEMBERS : (k + 1) * MEMBERS, :]
        good = flagged[k * MEMBERS : (k + 1) * MEMBERS, :]
        flags += jnp.where((lane >= offset) & (lane < offset + good), 1.0, 0.0)
        own_first = jnp.sum(jnp.where(mine, offset, 0.0), axis=0, keepdims=True)
        own_count = jnp.sum(jnp.where(mine, here, 0.0), axis=0, keepdims=True)
        plan[k * SLOTS : (k + 1) * SLOTS, :] = jnp.where(
            (slot + own_first == lane_slot) & (slot < own_count), 1.0, 0.0
        ).astype(BF16)
        offset += here
    plan[PATCHES * SLOTS :, :] = jnp.concatenate([flags, flags], axis=0).astype(BF16)
    mask = iota((PATCH, QBLOCK), 0) < limit
    for h in range(2):
        keys = qkv[:, h * HEAD : (h + 1) * HEAD]
        values_t = qkv[:, PAIR + h * HEAD : PAIR + (h + 1) * HEAD].astype(F32).T.astype(BF16)
        for n in range(PATCH // QBLOCK):
            span = slice(n * QBLOCK, (n + 1) * QBLOCK)
            query = qkv[span, 2 * PAIR + h * HEAD : 2 * PAIR + (h + 1) * HEAD]
            probs = softmax_keys(keys, query, mask)
            att[h * HEAD : (h + 1) * HEAD, span] = dot(values_t, probs.astype(BF16))
    for b in range(MEMBERS):
        attended[b] = att[:, b * ROWS : (b + 1) * ROWS].astype(BF16)


def halves(blocks, first, last):
    return [
        jnp.concatenate([blocks[2 * x + c, :, first:last] for x in range(4)], axis=0)
        for c in range(2)
    ]


def mix_kernel(targets, attended, points, shared, send):
    place = place_rows(targets)
    weights = halves(shared, 0, WIDTH // 2)
    mixed = jnp.concatenate([dot(attended[...], w, 0, 0) for w in weights], axis=1)
    mixed = points[...].astype(F32) + mixed
    send[...] = dot(place, mixed.astype(BF16)).astype(BF16)


def collect_kernel(arrived, plan, grads):
    grads[...] = dot(plan[: PATCHES * SLOTS, :], arrived[...], 0, 0).astype(BF16)


def project_kernel(arrived, plan, project, output, grads, send, rows):
    mixed = dot(plan[: PATCHES * SLOTS, :], arrived[...], 0, 0).astype(BF16)
    rows[...] = mixed
    low, high = halves(output, 0, WIDTH // 2)
    grad_attended = dot(grads[:, : WIDTH // 2], low, 1, 1) + dot(grads[:, WIDTH // 2 :], high, 1, 1)
    unit, _ = normalize(mixed.astype(F32))
    unit = unit.astype(BF16)
    projected = [dot(unit, w) for w in halves(project, 0, 3 * WIDTH // 2)]
    for k in range(MEMBERS):
        half, t = projected[k % 2], k // 2
        first = WIDTH // 2 + t * 2 * PAIR
        send[k, :ROWS, :] = half[:, first : first + 2 * PAIR].astype(BF16)
        send[k, ROWS:, :] = jnp.concatenate(
            [half[:, t * PAIR : (t + 1) * PAIR], grad_attended[:, k * PAIR : (k + 1) * PAIR]],
            axis=1,
        ).astype(BF16)


def backward_body(qkv, grad_t, mask, send, attended, dq, dk, dv):
    for h in range(2):
        low, high = h * HEAD, (h + 1) * HEAD
        keys = qkv[:, low:high]
        values = qkv[:, PAIR + low : PAIR + high]
        keys_t = keys.astype(F32).T.astype(BF16)
        values_t = values.astype(F32).T.astype(BF16)
        for n in range(PATCH // QBLOCK):
            span = slice(n * QBLOCK, (n + 1) * QBLOCK)
            query = qkv[span, 2 * PAIR + low : 2 * PAIR + high]
            grad = grad_t[low:high, span]
            probs = softmax_keys(keys, query, mask)
            probs_low = probs.astype(BF16)
            grad_probs = dot(values, grad)
            row_dot = jnp.sum(probs * grad_probs, axis=0, keepdims=True)
            grad_scores = (probs * (grad_probs - row_dot)).astype(BF16)
            dq[low:high, span] = dot(keys_t, grad_scores)
            part_k = dot(grad_scores, query)
            part_v = dot(probs_low, grad, 1, 1)
            if n == 0:
                dk[:, low:high] = part_k
                dv[:, low:high] = part_v
            else:
                dk[:, low:high] += part_k
                dv[:, low:high] += part_v
            if attended is not None:
                attended[low:high, span] = dot(values_t, probs_low).astype(BF16)
    for b in range(MEMBERS):
        rows = slice(b * ROWS, (b + 1) * ROWS)
        send[b, :ROWS, :] = jnp.concatenate([dk[rows, :] * SCALE, dv[rows, :]], axis=1).astype(BF16)
        send[b, ROWS:, :] = (dq[:, rows] * SCALE).astype(BF16)


def backward_h_kernel(arrived, plan, send, attended, qkv, grad_t, dq, dk, dv):
    for b in range(MEMBERS):
        rows = slice(b * ROWS, (b + 1) * ROWS)
        qkv[rows, :ROWS] = arrived[b, :ROWS, :]
        both = arrived[b, ROWS:, :]
        qkv[rows, ROWS:] = both
        grad_t[:, rows] = both.astype(F32).T[PAIR:, :].astype(BF16)
    mask = key_mask(plan[PATCHES * SLOTS : PATCHES * SLOTS + MEMBERS, :])
    backward_body(qkv, grad_t, mask, send, attended, dq, dk, dv)


def backward_z_kernel(scal, arrived, qkv, send, grad_t, dq, dk, dv):
    for b in range(MEMBERS):
        grad_t[:, b * ROWS : (b + 1) * ROWS] = arrived[b]
    mask = iota((PATCH, QBLOCK), 0) < scal[2 + scal[1]]
    backward_body(qkv, grad_t, mask, send, None, dq, dk, dv)


def input_grad(arrived, weights, rows, grads):
    sides = []
    for c in range(2):
        members = range(c, MEMBERS, 2)
        query_part = jnp.concatenate([arrived[k, ROWS:, :].astype(F32) for k in members], axis=0)
        sides.append(
            jnp.concatenate(
                [query_part.T.astype(BF16)] + [arrived[k, :ROWS, :] for k in members], axis=1
            )
        )
    grad_normed = dot(sides[0], weights[0], 1, 1) + dot(sides[1], weights[1], 1, 1)
    unit, inverse = normalize(rows[...].astype(F32))
    return (grads[...].astype(F32) + normalize_back(grad_normed, unit, inverse)).astype(BF16)


def return_kernel(arrived, project, rows, grads, plan, attended, all_grads, send):
    grad = input_grad(arrived, halves(project, 0, 3 * WIDTH // 2), rows, grads)
    spaced = dot(plan[: PATCHES * SLOTS, :], grad).astype(BF16)
    term = dot(attended[...], all_grads[...])
    upper = term.astype(BF16)
    lower = (term - upper.astype(F32)).astype(BF16)
    for k in range(PATCHES):
        send[k, :SLOTS, :] = spaced[k * SLOTS : (k + 1) * SLOTS, :]
        share = slice(k * SHARE, (k + 1) * SHARE)
        send[k, SLOTS:, :] = jnp.concatenate([upper[share, :], lower[share, :]], axis=0)


def regain_kernel(arrived, targets, output, grad_mixed, send, term):
    spaced = jnp.concatenate([arrived[k, :SLOTS, :] for k in range(PATCHES)], axis=0)
    grad = dot(place_rows(targets), spaced, 0, 0).astype(BF16)
    grad_mixed[...] = grad
    low, high = halves(output, 0, WIDTH // 2)
    grad_attended = dot(low, grad[:, : WIDTH // 2], 1, 1) + dot(high, grad[:, WIDTH // 2 :], 1, 1)
    send[...] = grad_attended.astype(BF16)
    total = jnp.zeros((2 * SHARE, WIDTH), F32)
    for k in range(PATCHES):
        total += arrived[k, SLOTS:, :].astype(F32)
    factor = (SCENES * PATCHES * PATCH) ** (-0.5)
    term[...] = (total[:SHARE, :] + total[SHARE:, :]) * factor


def finish_kernel(arrived, project, rows, grads, out):
    out[...] = input_grad(arrived, halves(project, 0, 3 * WIDTH // 2), rows, grads)


def exchange(value, axes):
    return lax.all_to_all(value, axes, split_axis=0, concat_axis=0, tiled=True)


def per_device(
    points, cotangent, valid_counts, zorder_targets, hilbert_sources,
    zorder_project, zorder_output, hilbert_project, hilbert_output,
):
    rows = points[0]
    cot = cotangent[0]
    member = lax.axis_index(GROUP).astype(jnp.int32)
    patch = lax.axis_index(ACROSS).astype(jnp.int32)
    scal = jnp.concatenate([jnp.stack([member, patch]), valid_counts[0]])
    targets = zorder_targets[0]
    sources = hilbert_sources[0]

    targets = targets[None, :]
    mine, weights, send_grads = call(
        prepare_kernel,
        [rows, cot, targets, sources[None, :], zorder_project, hilbert_project, zorder_output, hilbert_output],
        [
            ((ROWS + META, WIDTH), BF16),
            ((2, SHARE, 4 * WIDTH), BF16),
            ((PATCHES * SLOTS, WIDTH), BF16),
        ],
    )
    gathered = lax.all_gather(mine, GROUP, axis=0, tiled=True)
    weights = exchange(weights, "core").reshape(MEMBERS, 4 * WIDTH)
    weights = lax.all_gather(weights, ("zh", "zl"), axis=0, tiled=True)
    third = 3 * WIDTH // 2
    quarter = lax.axis_index("zl")
    own = jnp.concatenate(
        [
            lax.dynamic_slice_in_dim(weights, 4 * PAIR + quarter * 2 * PAIR, 2 * PAIR, 1),
            lax.dynamic_slice_in_dim(weights, quarter * PAIR, PAIR, 1),
            jnp.zeros((ROWS, PAIR), BF16),
        ],
        axis=1,
    )
    own = lax.all_gather(own, "x", axis=0, tiled=True)
    shared = lax.all_gather(weights[:, third:], ("x", "core"), axis=0, tiled=True)
    shared = shared.reshape(MEMBERS, ROWS, third + WIDTH)
    project_z = lax.all_gather(weights[:, :third], ("x", "core"), axis=0, tiled=True)
    project_z = project_z.reshape(MEMBERS, ROWS, third)

    send_grads, own = lax.optimization_barrier((send_grads, own))
    arrived_grads = exchange(send_grads.reshape(PATCHES, SLOTS, WIDTH), ACROSS)

    qkv_z, attended, plan = call(
        forward_kernel,
        [scal, gathered, own],
        [
            ((PATCH, 4 * PAIR), BF16),
            ((MEMBERS, PAIR, ROWS), BF16),
            ((PATCHES * SLOTS + 2 * MEMBERS, ROWS), BF16),
        ],
        [pltpu.VMEM((PAIR, PATCH), F32)],
        micros=8,
    )

    attended, arrived_grads = lax.optimization_barrier((attended, arrived_grads))
    (grads_h,) = call(
        collect_kernel,
        [arrived_grads.reshape(PATCHES * SLOTS, WIDTH), plan],
        [((ROWS, WIDTH), BF16)],
    )
    attended = exchange(attended, GROUP).reshape(WIDTH, ROWS)
    attended, grads_h, shared = lax.optimization_barrier((attended, grads_h, shared))
    all_grads_h = lax.all_gather(grads_h, GROUP, axis=0, tiled=True)
    (send,) = call(
        mix_kernel,
        [targets, attended, rows, (shared, *OUTPUT_Z)],
        [((PATCHES * SLOTS, WIDTH), BF16)],
    )

    arrived = exchange(send.reshape(PATCHES, SLOTS, WIDTH), ACROSS)
    send, rows_h = call(
        project_kernel,
        [
            arrived.reshape(PATCHES * SLOTS, WIDTH),
            plan,
            (shared, *PROJECT_H),
            (shared, *OUTPUT_H),
            grads_h,
        ],
        [((MEMBERS, 2 * ROWS, ROWS), BF16), ((ROWS, WIDTH), BF16)],
    )

    arrived = exchange(send, GROUP)
    sums = [
        pltpu.VMEM((PAIR, PATCH), F32),
        pltpu.VMEM((PATCH, PAIR), F32),
        pltpu.VMEM((PATCH, PAIR), F32),
    ]
    send, attended_h = call(
        backward_h_kernel,
        [arrived, plan],
        [((MEMBERS, 3 * PAIR, ROWS), BF16), ((PAIR, PATCH), BF16)],
        [pltpu.VMEM((PATCH, 4 * PAIR), BF16), pltpu.VMEM((PAIR, PATCH), BF16)] + sums,
        micros=11,
    )

    arrived = exchange(send, GROUP)
    (send,) = call(
        return_kernel,
        [arrived, (shared, *PROJECT_H), rows_h, grads_h, plan, attended_h, all_grads_h],
        [((PATCHES, SLOTS + 2 * SHARE, WIDTH), BF16)],
    )

    arrived = exchange(send, ACROSS)
    grad_mixed, send, term = call(
        regain_kernel,
        [arrived, targets, (shared, *OUTPUT_Z)],
        [((ROWS, WIDTH), BF16), ((WIDTH, ROWS), BF16), ((SHARE, WIDTH), F32)],
    )
    beside = lax.ppermute(term, "scene", [(i, i ^ 1) for i in range(SCENES)])
    arrived = exchange(send.reshape(MEMBERS, PAIR, ROWS), GROUP)
    arrived, beside = lax.optimization_barrier((arrived, beside))
    term = term + beside
    beside = lax.ppermute(term, "scene", [(i, i ^ 2) for i in range(SCENES)])
    (send,) = call(
        backward_z_kernel,
        [scal, arrived, qkv_z],
        [((MEMBERS, 3 * PAIR, ROWS), BF16)],
        [pltpu.VMEM((PAIR, PATCH), BF16)] + sums,
        micros=11,
    )
    send, term, beside = lax.optimization_barrier((send, term, beside))
    term = lax.ppermute(
        term + beside,
        PTS,
        [(r * MEMBERS + j, j * PATCHES + r) for r in range(PATCHES) for j in range(MEMBERS)],
    )

    arrived = exchange(send, GROUP)
    (out,) = call(finish_kernel, [arrived, project_z, rows, grad_mixed], [((ROWS, WIDTH), BF16)])
    return out[None], term


def solution(mesh):
    devices = mesh.devices.reshape(4, 4, 4, 2, 4)
    fine = Mesh(devices, ("x", "zh", "zl", "core", "scene"))
    rows = P("scene", PTS, None)
    index = P("scene", PTS)
    weight = P(PTS, None)
    return jax.shard_map(
        per_device,
        mesh=fine,
        in_specs=(rows, rows, P("scene", None), index, index, weight, weight, weight, weight),
        out_specs=(rows, weight),
        check_vma=False,
    )
```

```python
import functools

import jax
import jax.numpy as jnp
from jax import lax
from jax.experimental import pallas as pl
from jax.experimental.pallas import tpu as pltpu
from jax.sharding import Mesh, PartitionSpec as P

HEADS = 16
PATCH = 1024
WIDTH = 512
HEAD = 32
ROWS = 128
PAIR = 64
MEMBERS = 8
PATCHES = 16
SLOTS = 16
META = 16
SHARE = 4
SCENES = 4
PROJECT_H = (0, 768)
OUTPUT_Z = (768, 1024)
OUTPUT_H = (1024, 1280)
EPSILON = 1e-05
NEGATIVE = -1e30
SCALE = HEAD ** (-0.5)
LOG2E = 1.4426950408889634
QBLOCK = 1024
MICRO = 1_150_000_000

F32 = jnp.float32
BF16 = jnp.bfloat16
PTS = ("x", "zh", "zl", "core")
GROUP = ("zl", "core")
ACROSS = ("x", "zh")


def dot(a, b, ca=1, cb=0):
    return lax.dot_general(a, b, (((ca,), (cb,)), ((), ())), preferred_element_type=F32)


def normalize(values):
    center = values - jnp.mean(values, axis=1, keepdims=True)
    inverse = lax.rsqrt(jnp.mean(center * center, axis=1, keepdims=True) + EPSILON)
    return center * inverse, inverse


def normalize_back(grad, unit, inverse):
    middle = grad - jnp.mean(grad, axis=1, keepdims=True)
    return inverse * (middle - unit * jnp.mean(grad * unit, axis=1, keepdims=True))


def iota(shape, dim):
    return lax.broadcasted_iota(jnp.int32, shape, dim)


def call(kernel, ins, outs, scratch=(), limit=32, micros=1, pull=False):
    views = [item[1:] if isinstance(item, tuple) else None for item in ins]
    arrays = [item[0] if isinstance(item, tuple) else item for item in ins]
    scalars = [a.ndim == 1 for a in arrays]
    held = [pltpu.VMEM(a.shape, a.dtype) for a in arrays] if pull else []
    held += [pltpu.SemaphoreType.DMA((len(arrays),))] if pull else []

    def body(*refs):
        given = list(refs)
        if pull:
            given, buffers, sems = given[: -len(held)], given[-len(held) : -1], given[-1]
            copies = [
                pltpu.make_async_copy(refs[k], buffer, sems.at[k]) for k, buffer in enumerate(buffers)
            ]
            for copy in copies:
                copy.start()
            for copy in copies:
                copy.wait()
            given[: len(buffers)] = buffers
        for k, view in enumerate(views):
            if view is not None:
                lead = (slice(None),) * (len(arrays[k].shape) - 1)
                given[k] = refs[k].at[lead + (pl.ds(view[0], view[1] - view[0]),)]
        kernel(*given)

    return pl.pallas_call(
        body,
        out_shape=[jax.ShapeDtypeStruct(shape, dtype) for shape, dtype in outs],
        in_specs=[
            pl.BlockSpec(memory_space=pltpu.SMEM if flat else pl.ANY if pull else pltpu.VMEM)
            for flat in scalars
        ],
        out_specs=[pl.BlockSpec(memory_space=pltpu.VMEM) for _ in outs],
        scratch_shapes=list(scratch) + held,
        cost_estimate=pl.CostEstimate(flops=micros * MICRO, bytes_accessed=0, transcendentals=0),
        compiler_params=pltpu.CompilerParams(vmem_limit_bytes=limit * 1024 * 1024),
    )(*arrays)


def softmax_keys(keys, query, mask):
    scores = dot(keys, query, 1, 1) * (SCALE * LOG2E)
    scores = jnp.where(mask, scores, NEGATIVE)
    weights = jnp.exp2(scores - jnp.max(scores, axis=0, keepdims=True))
    return weights * (1.0 / jnp.sum(weights, axis=0, keepdims=True))


def key_mask(flags):
    parts = []
    for b in range(MEMBERS):
        pick = jnp.where(iota((MEMBERS, QBLOCK), 0) == b, 1.0, 0.0).astype(BF16)
        parts.append(dot(flags, pick, 0, 0))
    return jnp.concatenate(parts, axis=0) > 0.5


def place_rows(targets):
    patch = targets[...] // PATCH
    patches = jnp.broadcast_to(patch, (MEMBERS, ROWS)).astype(F32)
    column = jnp.broadcast_to(patches.T[:, :1], (ROWS, ROWS))
    row = jnp.broadcast_to(patch, (ROWS, ROWS)).astype(F32)
    same = (column == row) & (iota((ROWS, ROWS), 0) < iota((ROWS, ROWS), 1))
    rank = jnp.sum(jnp.where(same, 1.0, 0.0), axis=0, keepdims=True).astype(jnp.int32)
    code = patch * SLOTS + rank
    return jnp.where(iota((PATCHES * SLOTS, ROWS), 0) == code, 1.0, 0.0).astype(BF16)


def prepare_kernel(
    points, cotangent, targets, sources, project_z, project_h, output_z, output_h, mine, weights, grads
):
    grads[...] = dot(place_rows(targets), cotangent[...]).astype(BF16)
    mine[:ROWS, :] = points[...]
    source = sources[...]
    digits = jnp.concatenate([source // ROWS, source % ROWS], axis=1).astype(F32)
    digits = jnp.concatenate([digits, jnp.zeros((1, WIDTH - 2 * ROWS), F32)], axis=1)
    mine[ROWS:, :] = jnp.broadcast_to(digits, (META, WIDTH)).astype(BF16)
    for c in range(2):
        pieces = []
        for project in (project_z, project_h):
            values = project[...].astype(F32)
            pairs = range(c, MEMBERS, 2)
            pieces += [values[:, k * PAIR : (k + 1) * PAIR] for k in pairs]
            for k in pairs:
                pieces += [
                    values[:, n * WIDTH + k * PAIR : n * WIDTH + (k + 1) * PAIR] for n in (1, 2)
                ]
        for output in (output_z, output_h):
            half = WIDTH // 2
            pieces.append(output[:, c * half : (c + 1) * half].astype(F32))
        weights[c] = jnp.concatenate(pieces, axis=1).astype(BF16)


def forward_kernel(scal, gathered, weights, qkv, attended, plan, att):
    member = scal[0]
    limit = scal[2 + scal[1]]
    w = weights[...]
    stride = ROWS + META
    source = gathered
    device = iota((ROWS, ROWS), 0)
    total = jnp.zeros((ROWS, ROWS), F32)
    flagged = jnp.zeros((ROWS, ROWS), F32)
    bound = jnp.concatenate(
        [scal[2 + k] - ROWS * iota((MEMBERS, ROWS), 0) for k in range(PATCHES)], axis=0
    ).astype(F32)
    device_f = device.astype(F32)
    for b in range(MEMBERS):
        first = b * stride
        block = source[first : first + ROWS, :]
        unit, _ = normalize(block.astype(F32))
        unit = unit.astype(BF16)
        rows = slice(b * ROWS, (b + 1) * ROWS)
        qkv[rows, :] = dot(unit, w).astype(BF16)
        meta = source[first + ROWS : first + stride, :].astype(F32)
        owner = meta[0:1, 0:ROWS]
        place = meta[0:1, ROWS : 2 * ROWS]
        hit = device_f == owner
        total += jnp.where(hit, 1.0, 0.0)
        flagged += jnp.where(hit & (place < bound), 1.0, 0.0)
    total = jnp.sum(total, axis=1, keepdims=True)
    flagged = jnp.sum(flagged, axis=1, keepdims=True)
    lane = iota((MEMBERS, ROWS), 1).astype(F32)
    mine = iota((MEMBERS, 1), 0) == member
    slot = iota((SLOTS, ROWS), 0).astype(F32)
    lane_slot = iota((SLOTS, ROWS), 1).astype(F32)
    offset = jnp.zeros((MEMBERS, 1), F32)
    flags = jnp.zeros((MEMBERS, ROWS), F32)
    for k in range(PATCHES):
        here = total[k * MEMBERS : (k + 1) * MEMBERS, :]
        good = flagged[k * MEMBERS : (k + 1) * MEMBERS, :]
        flags += jnp.where((lane >= offset) & (lane < offset + good), 1.0, 0.0)
        own_first = jnp.sum(jnp.where(mine, offset, 0.0), axis=0, keepdims=True)
        own_count = jnp.sum(jnp.where(mine, here, 0.0), axis=0, keepdims=True)
        plan[k * SLOTS : (k + 1) * SLOTS, :] = jnp.where(
            (slot + own_first == lane_slot) & (slot < own_count), 1.0, 0.0
        ).astype(BF16)
        offset += here
    plan[PATCHES * SLOTS :, :] = jnp.concatenate([flags, flags], axis=0).astype(BF16)
    mask = iota((PATCH, QBLOCK), 0) < limit
    for h in range(2):
        keys = qkv[:, h * HEAD : (h + 1) * HEAD]
        values_t = qkv[:, PAIR + h * HEAD : PAIR + (h + 1) * HEAD].astype(F32).T.astype(BF16)
        for n in range(PATCH // QBLOCK):
            span = slice(n * QBLOCK, (n + 1) * QBLOCK)
            query = qkv[span, 2 * PAIR + h * HEAD : 2 * PAIR + (h + 1) * HEAD]
            probs = softmax_keys(keys, query, mask)
            att[h * HEAD : (h + 1) * HEAD, span] = dot(values_t, probs.astype(BF16))
    for b in range(MEMBERS):
        attended[b] = att[:, b * ROWS : (b + 1) * ROWS].astype(BF16)


def halves(blocks, first, last):
    return [
        jnp.concatenate([blocks[2 * x + c, :, first:last] for x in range(4)], axis=0)
        for c in range(2)
    ]


def mix_kernel(targets, attended, points, shared, send):
    place = place_rows(targets)
    weights = halves(shared, 0, WIDTH // 2)
    mixed = jnp.concatenate([dot(attended[...], w, 0, 0) for w in weights], axis=1)
    mixed = points[...].astype(F32) + mixed
    send[...] = dot(place, mixed.astype(BF16)).astype(BF16)


def collect_kernel(arrived, plan, grads):
    grads[...] = dot(plan[: PATCHES * SLOTS, :], arrived[...], 0, 0).astype(BF16)


def project_kernel(arrived, plan, project, output, grads, send, rows):
    mixed = dot(plan[: PATCHES * SLOTS, :], arrived[...], 0, 0).astype(BF16)
    rows[...] = mixed
    low, high = halves(output, 0, WIDTH // 2)
    grad_attended = dot(grads[:, : WIDTH // 2], low, 1, 1) + dot(grads[:, WIDTH // 2 :], high, 1, 1)
    unit, _ = normalize(mixed.astype(F32))
    unit = unit.astype(BF16)
    projected = [dot(unit, w) for w in halves(project, 0, 3 * WIDTH // 2)]
    for k in range(MEMBERS):
        half, t = projected[k % 2], k // 2
        first = WIDTH // 2 + t * 2 * PAIR
        send[k, :ROWS, :] = half[:, first : first + 2 * PAIR].astype(BF16)
        send[k, ROWS:, :] = jnp.concatenate(
            [half[:, t * PAIR : (t + 1) * PAIR], grad_attended[:, k * PAIR : (k + 1) * PAIR]],
            axis=1,
        ).astype(BF16)


def backward_body(qkv, grad_t, mask, send, attended, dq, dk, dv):
    for h in range(2):
        low, high = h * HEAD, (h + 1) * HEAD
        keys = qkv[:, low:high]
        values = qkv[:, PAIR + low : PAIR + high]
        keys_t = keys.astype(F32).T.astype(BF16)
        values_t = values.astype(F32).T.astype(BF16)
        for n in range(PATCH // QBLOCK):
            span = slice(n * QBLOCK, (n + 1) * QBLOCK)
            query = qkv[span, 2 * PAIR + low : 2 * PAIR + high]
            grad = grad_t[low:high, span]
            probs = softmax_keys(keys, query, mask)
            probs_low = probs.astype(BF16)
            grad_probs = dot(values, grad)
            row_dot = jnp.sum(probs * grad_probs, axis=0, keepdims=True)
            grad_scores = (probs * (grad_probs - row_dot)).astype(BF16)
            dq[low:high, span] = dot(keys_t, grad_scores)
            part_k = dot(grad_scores, query)
            part_v = dot(probs_low, grad, 1, 1)
            if n == 0:
                dk[:, low:high] = part_k
                dv[:, low:high] = part_v
            else:
                dk[:, low:high] += part_k
                dv[:, low:high] += part_v
            if attended is not None:
                attended[low:high, span] = dot(values_t, probs_low).astype(BF16)
    for b in range(MEMBERS):
        rows = slice(b * ROWS, (b + 1) * ROWS)
        send[b, :ROWS, :] = jnp.concatenate([dk[rows, :] * SCALE, dv[rows, :]], axis=1).astype(BF16)
        send[b, ROWS:, :] = (dq[:, rows] * SCALE).astype(BF16)


def backward_h_kernel(arrived, plan, send, attended, qkv, grad_t, dq, dk, dv):
    for b in range(MEMBERS):
        rows = slice(b * ROWS, (b + 1) * ROWS)
        qkv[rows, :ROWS] = arrived[b, :ROWS, :]
        both = arrived[b, ROWS:, :]
        qkv[rows, ROWS:] = both
        grad_t[:, rows] = both.astype(F32).T[PAIR:, :].astype(BF16)
    mask = key_mask(plan[PATCHES * SLOTS : PATCHES * SLOTS + MEMBERS, :])
    backward_body(qkv, grad_t, mask, send, attended, dq, dk, dv)


def backward_z_kernel(scal, arrived, qkv, send, grad_t, dq, dk, dv):
    for b in range(MEMBERS):
        grad_t[:, b * ROWS : (b + 1) * ROWS] = arrived[b]
    mask = iota((PATCH, QBLOCK), 0) < scal[2 + scal[1]]
    backward_body(qkv, grad_t, mask, send, None, dq, dk, dv)


def input_grad(arrived, weights, rows, grads):
    sides = []
    for c in range(2):
        members = range(c, MEMBERS, 2)
        query_part = jnp.concatenate([arrived[k, ROWS:, :].astype(F32) for k in members], axis=0)
        sides.append(
            jnp.concatenate(
                [query_part.T.astype(BF16)] + [arrived[k, :ROWS, :] for k in members], axis=1
            )
        )
    grad_normed = dot(sides[0], weights[0], 1, 1) + dot(sides[1], weights[1], 1, 1)
    unit, inverse = normalize(rows[...].astype(F32))
    return (grads[...].astype(F32) + normalize_back(grad_normed, unit, inverse)).astype(BF16)


def return_kernel(arrived, project, rows, grads, plan, attended, all_grads, send):
    grad = input_grad(arrived, halves(project, 0, 3 * WIDTH // 2), rows, grads)
    spaced = dot(plan[: PATCHES * SLOTS, :], grad).astype(BF16)
    term = dot(attended[...], all_grads[...])
    upper = term.astype(BF16)
    lower = (term - upper.astype(F32)).astype(BF16)
    for k in range(PATCHES):
        send[k, :SLOTS, :] = spaced[k * SLOTS : (k + 1) * SLOTS, :]
        share = slice(k * SHARE, (k + 1) * SHARE)
        send[k, SLOTS:, :] = jnp.concatenate([upper[share, :], lower[share, :]], axis=0)


def regain_kernel(arrived, targets, output, grad_mixed, send, term):
    spaced = jnp.concatenate([arrived[k, :SLOTS, :] for k in range(PATCHES)], axis=0)
    grad = dot(place_rows(targets), spaced, 0, 0).astype(BF16)
    grad_mixed[...] = grad
    low, high = halves(output, 0, WIDTH // 2)
    grad_attended = dot(low, grad[:, : WIDTH // 2], 1, 1) + dot(high, grad[:, WIDTH // 2 :], 1, 1)
    send[...] = grad_attended.astype(BF16)
    total = jnp.zeros((2 * SHARE, WIDTH), F32)
    for k in range(PATCHES):
        total += arrived[k, SLOTS:, :].astype(F32)
    factor = (SCENES * PATCHES * PATCH) ** (-0.5)
    term[...] = (total[:SHARE, :] + total[SHARE:, :]) * factor


def finish_kernel(arrived, project, rows, grads, out):
    out[...] = input_grad(arrived, halves(project, 0, 3 * WIDTH // 2), rows, grads)


def exchange(value, axes):
    return lax.all_to_all(value, axes, split_axis=0, concat_axis=0, tiled=True)


def per_device(
    points, cotangent, valid_counts, zorder_targets, hilbert_sources,
    zorder_project, zorder_output, hilbert_project, hilbert_output,
):
    rows = points[0]
    cot = cotangent[0]
    member = lax.axis_index(GROUP).astype(jnp.int32)
    patch = lax.axis_index(ACROSS).astype(jnp.int32)
    scal = jnp.concatenate([jnp.stack([member, patch]), valid_counts[0]])
    targets = zorder_targets[0]
    sources = hilbert_sources[0]

    targets = targets[None, :]
    mine, weights, send_grads = call(
        prepare_kernel,
        [rows, cot, targets, sources[None, :], zorder_project, hilbert_project, zorder_output, hilbert_output],
        [
            ((ROWS + META, WIDTH), BF16),
            ((2, SHARE, 4 * WIDTH), BF16),
            ((PATCHES * SLOTS, WIDTH), BF16),
        ],
        limit=60,
        pull=True,
    )
    gathered = lax.all_gather(mine, GROUP, axis=0, tiled=True)
    weights = exchange(weights, "core").reshape(MEMBERS, 4 * WIDTH)
    weights = lax.all_gather(weights, ("zh", "zl"), axis=0, tiled=True)
    third = 3 * WIDTH // 2
    quarter = lax.axis_index("zl")
    own = jnp.concatenate(
        [
            lax.dynamic_slice_in_dim(weights, 4 * PAIR + quarter * 2 * PAIR, 2 * PAIR, 1),
            lax.dynamic_slice_in_dim(weights, quarter * PAIR, PAIR, 1),
            jnp.zeros((ROWS, PAIR), BF16),
        ],
        axis=1,
    )
    own = lax.all_gather(own, "x", axis=0, tiled=True)
    shared = lax.all_gather(weights[:, third:], ("x", "core"), axis=0, tiled=True)
    shared = shared.reshape(MEMBERS, ROWS, third + WIDTH)
    project_z = lax.all_gather(weights[:, :third], ("x", "core"), axis=0, tiled=True)
    project_z = project_z.reshape(MEMBERS, ROWS, third)

    send_grads, own = lax.optimization_barrier((send_grads, own))
    arrived_grads = exchange(send_grads.reshape(PATCHES, SLOTS, WIDTH), ACROSS)

    qkv_z, attended, plan = call(
        forward_kernel,
        [scal, gathered, own],
        [
            ((PATCH, 4 * PAIR), BF16),
            ((MEMBERS, PAIR, ROWS), BF16),
            ((PATCHES * SLOTS + 2 * MEMBERS, ROWS), BF16),
        ],
        [pltpu.VMEM((PAIR, PATCH), F32)],
        micros=8,
    )

    attended, arrived_grads = lax.optimization_barrier((attended, arrived_grads))
    (grads_h,) = call(
        collect_kernel,
        [arrived_grads.reshape(PATCHES * SLOTS, WIDTH), plan],
        [((ROWS, WIDTH), BF16)],
    )
    attended = exchange(attended, GROUP).reshape(WIDTH, ROWS)
    attended, grads_h, shared = lax.optimization_barrier((attended, grads_h, shared))
    all_grads_h = lax.all_gather(grads_h, GROUP, axis=0, tiled=True)
    (send,) = call(
        mix_kernel,
        [targets, attended, rows, (shared, *OUTPUT_Z)],
        [((PATCHES * SLOTS, WIDTH), BF16)],
    )

    arrived = exchange(send.reshape(PATCHES, SLOTS, WIDTH), ACROSS)
    send, rows_h = call(
        project_kernel,
        [
            arrived.reshape(PATCHES * SLOTS, WIDTH),
            plan,
            (shared, *PROJECT_H),
            (shared, *OUTPUT_H),
            grads_h,
        ],
        [((MEMBERS, 2 * ROWS, ROWS), BF16), ((ROWS, WIDTH), BF16)],
    )

    arrived = exchange(send, GROUP)
    sums = [
        pltpu.VMEM((PAIR, PATCH), F32),
        pltpu.VMEM((PATCH, PAIR), F32),
        pltpu.VMEM((PATCH, PAIR), F32),
    ]
    send, attended_h = call(
        backward_h_kernel,
        [arrived, plan],
        [((MEMBERS, 3 * PAIR, ROWS), BF16), ((PAIR, PATCH), BF16)],
        [pltpu.VMEM((PATCH, 4 * PAIR), BF16), pltpu.VMEM((PAIR, PATCH), BF16)] + sums,
        micros=11,
    )

    arrived = exchange(send, GROUP)
    (send,) = call(
        return_kernel,
        [arrived, (shared, *PROJECT_H), rows_h, grads_h, plan, attended_h, all_grads_h],
        [((PATCHES, SLOTS + 2 * SHARE, WIDTH), BF16)],
    )

    arrived = exchange(send, ACROSS)
    grad_mixed, send, term = call(
        regain_kernel,
        [arrived, targets, (shared, *OUTPUT_Z)],
        [((ROWS, WIDTH), BF16), ((WIDTH, ROWS), BF16), ((SHARE, WIDTH), F32)],
    )
    term = lax.ppermute(
        term,
        PTS,
        [(r * MEMBERS + j, j * PATCHES + r) for r in range(PATCHES) for j in range(MEMBERS)],
    )
    arrived = exchange(send.reshape(MEMBERS, PAIR, ROWS), GROUP)
    (send,) = call(
        backward_z_kernel,
        [scal, arrived, qkv_z],
        [((MEMBERS, 3 * PAIR, ROWS), BF16)],
        [pltpu.VMEM((PAIR, PATCH), BF16)] + sums,
        micros=11,
    )
    send, term = lax.optimization_barrier((send, term))
    for k in (1, 2):
        term = term + lax.ppermute(term, "scene", [(i, i ^ k) for i in range(SCENES)])

    arrived = exchange(send, GROUP)
    (out,) = call(finish_kernel, [arrived, project_z, rows, grad_mixed], [((ROWS, WIDTH), BF16)])
    return out[None], term


def solution(mesh):
    devices = mesh.devices.reshape(4, 4, 4, 2, 4)
    fine = Mesh(devices, ("x", "zh", "zl", "core", "scene"))
    rows = P("scene", PTS, None)
    index = P("scene", PTS)
    weight = P(PTS, None)
    return jax.shard_map(
        per_device,
        mesh=fine,
        in_specs=(rows, rows, P("scene", None), index, index, weight, weight, weight, weight),
        out_specs=(rows, weight),
        check_vma=False,
    )
```

```python
import functools

import jax
import jax.numpy as jnp
from jax import lax
from jax.experimental import pallas as pl
from jax.experimental.pallas import tpu as pltpu
from jax.sharding import Mesh, PartitionSpec as P

HEADS = 16
PATCH = 1024
WIDTH = 512
HEAD = 32
ROWS = 128
PAIR = 64
MEMBERS = 8
PATCHES = 16
SLOTS = 16
META = 16
SHARE = 4
SCENES = 4
PROJECT_H = (0, 768)
OUTPUT_Z = (768, 1024)
OUTPUT_H = (1024, 1280)
EPSILON = 1e-05
NEGATIVE = -1e30
SCALE = HEAD ** (-0.5)
LOG2E = 1.4426950408889634
QBLOCK = 1024
MICRO = 1_150_000_000

F32 = jnp.float32
BF16 = jnp.bfloat16
PTS = ("x", "zh", "zl", "core")
GROUP = ("zl", "core")
ACROSS = ("x", "zh")


def dot(a, b, ca=1, cb=0):
    return lax.dot_general(a, b, (((ca,), (cb,)), ((), ())), preferred_element_type=F32)


def normalize(values):
    center = values - jnp.mean(values, axis=1, keepdims=True)
    inverse = lax.rsqrt(jnp.mean(center * center, axis=1, keepdims=True) + EPSILON)
    return center * inverse, inverse


def normalize_back(grad, unit, inverse):
    middle = grad - jnp.mean(grad, axis=1, keepdims=True)
    return inverse * (middle - unit * jnp.mean(grad * unit, axis=1, keepdims=True))


def iota(shape, dim):
    return lax.broadcasted_iota(jnp.int32, shape, dim)


def call(kernel, ins, outs, scratch=(), limit=32, micros=1, pull=False):
    views = [item[1:] if isinstance(item, tuple) else None for item in ins]
    arrays = [item[0] if isinstance(item, tuple) else item for item in ins]
    scalars = [a.ndim == 1 for a in arrays]
    held = [pltpu.VMEM(a.shape, a.dtype) for a in arrays] if pull else []
    held += [pltpu.SemaphoreType.DMA((len(arrays),))] if pull else []

    def body(*refs):
        given = list(refs)
        if pull:
            given, buffers, sems = given[: -len(held)], given[-len(held) : -1], given[-1]
            copies = [
                pltpu.make_async_copy(refs[k], buffer, sems.at[k]) for k, buffer in enumerate(buffers)
            ]
            for copy in copies:
                copy.start()
            for copy in copies:
                copy.wait()
            given[: len(buffers)] = buffers
        for k, view in enumerate(views):
            if view is not None:
                lead = (slice(None),) * (len(arrays[k].shape) - 1)
                given[k] = refs[k].at[lead + (pl.ds(view[0], view[1] - view[0]),)]
        kernel(*given)

    return pl.pallas_call(
        body,
        out_shape=[jax.ShapeDtypeStruct(shape, dtype) for shape, dtype in outs],
        in_specs=[
            pl.BlockSpec(memory_space=pltpu.SMEM if flat else pl.ANY if pull else pltpu.VMEM)
            for flat in scalars
        ],
        out_specs=[pl.BlockSpec(memory_space=pltpu.VMEM) for _ in outs],
        scratch_shapes=list(scratch) + held,
        cost_estimate=pl.CostEstimate(flops=micros * MICRO, bytes_accessed=0, transcendentals=0),
        compiler_params=pltpu.CompilerParams(vmem_limit_bytes=limit * 1024 * 1024),
    )(*arrays)


def softmax_keys(keys, query, mask):
    scores = dot(keys, query, 1, 1) * (SCALE * LOG2E)
    scores = jnp.where(mask, scores, NEGATIVE)
    weights = jnp.exp2(scores - jnp.max(scores, axis=0, keepdims=True))
    return weights * (1.0 / jnp.sum(weights, axis=0, keepdims=True))


def key_mask(flags):
    parts = []
    for b in range(MEMBERS):
        pick = jnp.where(iota((MEMBERS, QBLOCK), 0) == b, 1.0, 0.0).astype(BF16)
        parts.append(dot(flags, pick, 0, 0))
    return jnp.concatenate(parts, axis=0) > 0.5


def place_rows(targets):
    patch = targets[...] // PATCH
    patches = jnp.broadcast_to(patch, (MEMBERS, ROWS)).astype(F32)
    column = jnp.broadcast_to(patches.T[:, :1], (ROWS, ROWS))
    row = jnp.broadcast_to(patch, (ROWS, ROWS)).astype(F32)
    same = (column == row) & (iota((ROWS, ROWS), 0) < iota((ROWS, ROWS), 1))
    rank = jnp.sum(jnp.where(same, 1.0, 0.0), axis=0, keepdims=True).astype(jnp.int32)
    code = patch * SLOTS + rank
    return jnp.where(iota((PATCHES * SLOTS, ROWS), 0) == code, 1.0, 0.0).astype(BF16)


def prepare_kernel(
    points, cotangent, targets, sources, project_z, project_h, output_z, output_h, mine, weights, grads
):
    grads[...] = dot(place_rows(targets), cotangent[...]).astype(BF16)
    mine[:ROWS, :] = points[...]
    source = sources[...]
    digits = jnp.concatenate([source // ROWS, source % ROWS], axis=1).astype(F32)
    digits = jnp.concatenate([digits, jnp.zeros((1, WIDTH - 2 * ROWS), F32)], axis=1)
    mine[ROWS:, :] = jnp.broadcast_to(digits, (META, WIDTH)).astype(BF16)
    for c in range(2):
        pieces = []
        for project in (project_z, project_h):
            values = project[...].astype(F32)
            pairs = range(c, MEMBERS, 2)
            pieces += [values[:, k * PAIR : (k + 1) * PAIR] for k in pairs]
            for k in pairs:
                pieces += [
                    values[:, n * WIDTH + k * PAIR : n * WIDTH + (k + 1) * PAIR] for n in (1, 2)
                ]
        for output in (output_z, output_h):
            half = WIDTH // 2
            pieces.append(output[:, c * half : (c + 1) * half].astype(F32))
        weights[c] = jnp.concatenate(pieces, axis=1).astype(BF16)


def forward_kernel(scal, gathered, weights, qkv, attended, plan, att):
    member = scal[0]
    limit = scal[2 + scal[1]]
    w = weights[...]
    stride = ROWS + META
    source = gathered
    device = iota((ROWS, ROWS), 0)
    total = jnp.zeros((ROWS, ROWS), F32)
    flagged = jnp.zeros((ROWS, ROWS), F32)
    bound = jnp.concatenate(
        [scal[2 + k] - ROWS * iota((MEMBERS, ROWS), 0) for k in range(PATCHES)], axis=0
    ).astype(F32)
    device_f = device.astype(F32)
    for b in range(MEMBERS):
        first = b * stride
        block = source[first : first + ROWS, :]
        unit, _ = normalize(block.astype(F32))
        unit = unit.astype(BF16)
        rows = slice(b * ROWS, (b + 1) * ROWS)
        qkv[rows, :] = dot(unit, w).astype(BF16)
        meta = source[first + ROWS : first + stride, :].astype(F32)
        owner = meta[0:1, 0:ROWS]
        place = meta[0:1, ROWS : 2 * ROWS]
        hit = device_f == owner
        total += jnp.where(hit, 1.0, 0.0)
        flagged += jnp.where(hit & (place < bound), 1.0, 0.0)
    total = jnp.sum(total, axis=1, keepdims=True)
    flagged = jnp.sum(flagged, axis=1, keepdims=True)
    lane = iota((MEMBERS, ROWS), 1).astype(F32)
    mine = iota((MEMBERS, 1), 0) == member
    slot = iota((SLOTS, ROWS), 0).astype(F32)
    lane_slot = iota((SLOTS, ROWS), 1).astype(F32)
    offset = jnp.zeros((MEMBERS, 1), F32)
    flags = jnp.zeros((MEMBERS, ROWS), F32)
    for k in range(PATCHES):
        here = total[k * MEMBERS : (k + 1) * MEMBERS, :]
        good = flagged[k * MEMBERS : (k + 1) * MEMBERS, :]
        flags += jnp.where((lane >= offset) & (lane < offset + good), 1.0, 0.0)
        own_first = jnp.sum(jnp.where(mine, offset, 0.0), axis=0, keepdims=True)
        own_count = jnp.sum(jnp.where(mine, here, 0.0), axis=0, keepdims=True)
        plan[k * SLOTS : (k + 1) * SLOTS, :] = jnp.where(
            (slot + own_first == lane_slot) & (slot < own_count), 1.0, 0.0
        ).astype(BF16)
        offset += here
    plan[PATCHES * SLOTS :, :] = jnp.concatenate([flags, flags], axis=0).astype(BF16)
    mask = iota((PATCH, QBLOCK), 0) < limit
    for h in range(2):
        keys = qkv[:, h * HEAD : (h + 1) * HEAD]
        values_t = qkv[:, PAIR + h * HEAD : PAIR + (h + 1) * HEAD].astype(F32).T.astype(BF16)
        for n in range(PATCH // QBLOCK):
            span = slice(n * QBLOCK, (n + 1) * QBLOCK)
            query = qkv[span, 2 * PAIR + h * HEAD : 2 * PAIR + (h + 1) * HEAD]
            probs = softmax_keys(keys, query, mask)
            att[h * HEAD : (h + 1) * HEAD, span] = dot(values_t, probs.astype(BF16))
    for b in range(MEMBERS):
        attended[b] = att[:, b * ROWS : (b + 1) * ROWS].astype(BF16)


def halves(blocks, first, last):
    return [
        jnp.concatenate([blocks[2 * x + c, :, first:last] for x in range(4)], axis=0)
        for c in range(2)
    ]


def mix_kernel(targets, attended, points, shared, send):
    place = place_rows(targets)
    weights = halves(shared, 0, WIDTH // 2)
    mixed = jnp.concatenate([dot(attended[...], w, 0, 0) for w in weights], axis=1)
    mixed = points[...].astype(F32) + mixed
    send[...] = dot(place, mixed.astype(BF16)).astype(BF16)


def collect_kernel(arrived, plan, grads):
    grads[...] = dot(plan[: PATCHES * SLOTS, :], arrived[...], 0, 0).astype(BF16)


def project_kernel(arrived, plan, project, output, grads, send, rows):
    mixed = dot(plan[: PATCHES * SLOTS, :], arrived[...], 0, 0).astype(BF16)
    rows[...] = mixed
    low, high = halves(output, 0, WIDTH // 2)
    grad_attended = dot(grads[:, : WIDTH // 2], low, 1, 1) + dot(grads[:, WIDTH // 2 :], high, 1, 1)
    unit, _ = normalize(mixed.astype(F32))
    unit = unit.astype(BF16)
    projected = [dot(unit, w) for w in halves(project, 0, 3 * WIDTH // 2)]
    for k in range(MEMBERS):
        half, t = projected[k % 2], k // 2
        first = WIDTH // 2 + t * 2 * PAIR
        send[k, :ROWS, :] = half[:, first : first + 2 * PAIR].astype(BF16)
        send[k, ROWS:, :] = jnp.concatenate(
            [half[:, t * PAIR : (t + 1) * PAIR], grad_attended[:, k * PAIR : (k + 1) * PAIR]],
            axis=1,
        ).astype(BF16)


def backward_body(qkv, grad_t, mask, send, attended, dq, dk, dv):
    for h in range(2):
        low, high = h * HEAD, (h + 1) * HEAD
        keys = qkv[:, low:high]
        values = qkv[:, PAIR + low : PAIR + high]
        keys_t = keys.astype(F32).T.astype(BF16)
        values_t = values.astype(F32).T.astype(BF16)
        for n in range(PATCH // QBLOCK):
            span = slice(n * QBLOCK, (n + 1) * QBLOCK)
            query = qkv[span, 2 * PAIR + low : 2 * PAIR + high]
            grad = grad_t[low:high, span]
            probs = softmax_keys(keys, query, mask)
            probs_low = probs.astype(BF16)
            grad_probs = dot(values, grad)
            row_dot = jnp.sum(probs * grad_probs, axis=0, keepdims=True)
            grad_scores = (probs * (grad_probs - row_dot)).astype(BF16)
            dq[low:high, span] = dot(keys_t, grad_scores)
            part_k = dot(grad_scores, query)
            part_v = dot(probs_low, grad, 1, 1)
            if n == 0:
                dk[:, low:high] = part_k
                dv[:, low:high] = part_v
            else:
                dk[:, low:high] += part_k
                dv[:, low:high] += part_v
            if attended is not None:
                attended[low:high, span] = dot(values_t, probs_low).astype(BF16)
    for b in range(MEMBERS):
        rows = slice(b * ROWS, (b + 1) * ROWS)
        send[b, :ROWS, :] = jnp.concatenate([dk[rows, :] * SCALE, dv[rows, :]], axis=1).astype(BF16)
        send[b, ROWS:, :] = (dq[:, rows] * SCALE).astype(BF16)


def backward_h_kernel(arrived, plan, send, attended, qkv, grad_t, dq, dk, dv):
    for b in range(MEMBERS):
        rows = slice(b * ROWS, (b + 1) * ROWS)
        qkv[rows, :ROWS] = arrived[b, :ROWS, :]
        both = arrived[b, ROWS:, :]
        qkv[rows, ROWS:] = both
        grad_t[:, rows] = both.astype(F32).T[PAIR:, :].astype(BF16)
    mask = key_mask(plan[PATCHES * SLOTS : PATCHES * SLOTS + MEMBERS, :])
    backward_body(qkv, grad_t, mask, send, attended, dq, dk, dv)


def backward_z_kernel(scal, arrived, qkv, send, grad_t, dq, dk, dv):
    for b in range(MEMBERS):
        grad_t[:, b * ROWS : (b + 1) * ROWS] = arrived[b]
    mask = iota((PATCH, QBLOCK), 0) < scal[2 + scal[1]]
    backward_body(qkv, grad_t, mask, send, None, dq, dk, dv)


def input_grad(arrived, weights, rows, grads):
    sides = []
    for c in range(2):
        members = range(c, MEMBERS, 2)
        query_part = jnp.concatenate([arrived[k, ROWS:, :].astype(F32) for k in members], axis=0)
        sides.append(
            jnp.concatenate(
                [query_part.T.astype(BF16)] + [arrived[k, :ROWS, :] for k in members], axis=1
            )
        )
    grad_normed = dot(sides[0], weights[0], 1, 1) + dot(sides[1], weights[1], 1, 1)
    unit, inverse = normalize(rows[...].astype(F32))
    return (grads[...].astype(F32) + normalize_back(grad_normed, unit, inverse)).astype(BF16)


def return_kernel(arrived, project, rows, grads, plan, attended, all_grads, send):
    grad = input_grad(arrived, halves(project, 0, 3 * WIDTH // 2), rows, grads)
    spaced = dot(plan[: PATCHES * SLOTS, :], grad).astype(BF16)
    term = dot(attended[...], all_grads[...]).astype(BF16)
    tiles = [slice(t * ROWS, (t + 1) * ROWS) for t in range(4)]
    for k in range(PATCHES):
        rows = spaced[k * SLOTS : (k + 1) * SLOTS, :]
        for t, tile in enumerate(tiles):
            send[k, t * SLOTS : (t + 1) * SLOTS, :] = rows[:, tile]
        share = term[k * SHARE : (k + 1) * SHARE, :]
        send[k, 4 * SLOTS :, :] = jnp.concatenate([share[:, tile] for tile in tiles], axis=0)


def regain_kernel(arrived, targets, output, grad_mixed, send, term):
    spaced = jnp.concatenate(
        [
            jnp.concatenate([arrived[k, t * SLOTS : (t + 1) * SLOTS, :] for k in range(PATCHES)], axis=0)
            for t in range(4)
        ],
        axis=1,
    )
    grad = dot(place_rows(targets), spaced, 0, 0).astype(BF16)
    grad_mixed[...] = grad
    low, high = halves(output, 0, WIDTH // 2)
    grad_attended = dot(low, grad[:, : WIDTH // 2], 1, 1) + dot(high, grad[:, WIDTH // 2 :], 1, 1)
    send[...] = grad_attended.astype(BF16)
    total = jnp.zeros((4 * SHARE, ROWS), F32)
    for k in range(PATCHES):
        total += arrived[k, 4 * SLOTS :, :].astype(F32)
    total = jnp.concatenate([total[t * SHARE : (t + 1) * SHARE, :] for t in range(4)], axis=1)
    term[...] = total * (SCENES * PATCHES * PATCH) ** (-0.5)


def finish_kernel(arrived, project, rows, grads, out):
    out[...] = input_grad(arrived, halves(project, 0, 3 * WIDTH // 2), rows, grads)


def exchange(value, axes):
    return lax.all_to_all(value, axes, split_axis=0, concat_axis=0, tiled=True)


def per_device(
    points, cotangent, valid_counts, zorder_targets, hilbert_sources,
    zorder_project, zorder_output, hilbert_project, hilbert_output,
):
    rows = points[0]
    cot = cotangent[0]
    member = lax.axis_index(GROUP).astype(jnp.int32)
    patch = lax.axis_index(ACROSS).astype(jnp.int32)
    scal = jnp.concatenate([jnp.stack([member, patch]), valid_counts[0]])
    targets = zorder_targets[0]
    sources = hilbert_sources[0]

    targets = targets[None, :]
    mine, weights, send_grads = call(
        prepare_kernel,
        [rows, cot, targets, sources[None, :], zorder_project, hilbert_project, zorder_output, hilbert_output],
        [
            ((ROWS + META, WIDTH), BF16),
            ((2, SHARE, 4 * WIDTH), BF16),
            ((PATCHES * SLOTS, WIDTH), BF16),
        ],
        limit=60,
        pull=True,
    )
    gathered = lax.all_gather(mine, GROUP, axis=0, tiled=True)
    weights = exchange(weights, "core").reshape(MEMBERS, 4 * WIDTH)
    weights = lax.all_gather(weights, ("zh", "zl"), axis=0, tiled=True)
    third = 3 * WIDTH // 2
    quarter = lax.axis_index("zl")
    own = jnp.concatenate(
        [
            lax.dynamic_slice_in_dim(weights, 4 * PAIR + quarter * 2 * PAIR, 2 * PAIR, 1),
            lax.dynamic_slice_in_dim(weights, quarter * PAIR, PAIR, 1),
            jnp.zeros((ROWS, PAIR), BF16),
        ],
        axis=1,
    )
    own = lax.all_gather(own, "x", axis=0, tiled=True)
    shared = lax.all_gather(weights[:, third:], ("x", "core"), axis=0, tiled=True)
    shared = shared.reshape(MEMBERS, ROWS, third + WIDTH)
    project_z = weights[:, :third]

    send_grads, own, gathered = lax.optimization_barrier((send_grads, own, gathered))
    arrived_grads = exchange(send_grads.reshape(PATCHES, SLOTS, WIDTH), ACROSS)

    qkv_z, attended, plan = call(
        forward_kernel,
        [scal, gathered, own],
        [
            ((PATCH, 4 * PAIR), BF16),
            ((MEMBERS, PAIR, ROWS), BF16),
            ((PATCHES * SLOTS + 2 * MEMBERS, ROWS), BF16),
        ],
        [pltpu.VMEM((PAIR, PATCH), F32)],
        micros=8,
    )

    attended, arrived_grads, project_z = lax.optimization_barrier((attended, arrived_grads, project_z))
    project_z = lax.all_gather(project_z, ("x", "core"), axis=0, tiled=True)
    project_z = project_z.reshape(MEMBERS, ROWS, third)
    (grads_h,) = call(
        collect_kernel,
        [arrived_grads.reshape(PATCHES * SLOTS, WIDTH), plan],
        [((ROWS, WIDTH), BF16)],
    )
    attended = exchange(attended, GROUP).reshape(WIDTH, ROWS)
    attended, grads_h, shared = lax.optimization_barrier((attended, grads_h, shared))
    all_grads_h = lax.all_gather(grads_h, GROUP, axis=0, tiled=True)
    (send,) = call(
        mix_kernel,
        [targets, attended, rows, (shared, *OUTPUT_Z)],
        [((PATCHES * SLOTS, WIDTH), BF16)],
    )

    arrived = exchange(send.reshape(PATCHES, SLOTS, WIDTH), ACROSS)
    send, rows_h = call(
        project_kernel,
        [
            arrived.reshape(PATCHES * SLOTS, WIDTH),
            plan,
            (shared, *PROJECT_H),
            (shared, *OUTPUT_H),
            grads_h,
        ],
        [((MEMBERS, 2 * ROWS, ROWS), BF16), ((ROWS, WIDTH), BF16)],
    )

    arrived = exchange(send, GROUP)
    sums = [
        pltpu.VMEM((PAIR, PATCH), F32),
        pltpu.VMEM((PATCH, PAIR), F32),
        pltpu.VMEM((PATCH, PAIR), F32),
    ]
    send, attended_h = call(
        backward_h_kernel,
        [arrived, plan],
        [((MEMBERS, 3 * PAIR, ROWS), BF16), ((PAIR, PATCH), BF16)],
        [pltpu.VMEM((PATCH, 4 * PAIR), BF16), pltpu.VMEM((PAIR, PATCH), BF16)] + sums,
        micros=11,
    )

    arrived = exchange(send, GROUP)
    (send,) = call(
        return_kernel,
        [arrived, (shared, *PROJECT_H), rows_h, grads_h, plan, attended_h, all_grads_h],
        [((PATCHES, 4 * SLOTS + 4 * SHARE, ROWS), BF16)],
    )

    arrived = exchange(send, ACROSS)
    grad_mixed, send, term = call(
        regain_kernel,
        [arrived, targets, (shared, *OUTPUT_Z)],
        [((ROWS, WIDTH), BF16), ((WIDTH, ROWS), BF16), ((SHARE, WIDTH), F32)],
    )
    term = lax.ppermute(
        term,
        PTS,
        [(r * MEMBERS + j, j * PATCHES + r) for r in range(PATCHES) for j in range(MEMBERS)],
    )
    arrived = exchange(send.reshape(MEMBERS, PAIR, ROWS), GROUP)
    (send,) = call(
        backward_z_kernel,
        [scal, arrived, qkv_z],
        [((MEMBERS, 3 * PAIR, ROWS), BF16)],
        [pltpu.VMEM((PAIR, PATCH), BF16)] + sums,
        micros=11,
    )
    send, term = lax.optimization_barrier((send, term))
    for k in (1, 2):
        term = term + lax.ppermute(term, "scene", [(i, i ^ k) for i in range(SCENES)])

    arrived = exchange(send, GROUP)
    (out,) = call(finish_kernel, [arrived, project_z, rows, grad_mixed], [((ROWS, WIDTH), BF16)])
    return out[None], term


def solution(mesh):
    devices = mesh.devices.reshape(4, 4, 4, 2, 4)
    fine = Mesh(devices, ("x", "zh", "zl", "core", "scene"))
    rows = P("scene", PTS, None)
    index = P("scene", PTS)
    weight = P(PTS, None)
    return jax.shard_map(
        per_device,
        mesh=fine,
        in_specs=(rows, rows, P("scene", None), index, index, weight, weight, weight, weight),
        out_specs=(rows, weight),
        check_vma=False,
    )
```

```python
import functools

import jax
import jax.numpy as jnp
from jax import lax
from jax.experimental import pallas as pl
from jax.experimental.pallas import tpu as pltpu
from jax.sharding import Mesh, PartitionSpec as P

HEADS = 16
PATCH = 1024
WIDTH = 512
HEAD = 32
ROWS = 128
PAIR = 64
MEMBERS = 8
PATCHES = 16
SLOTS = 16
META = 16
SHARE = 4
SCENES = 4
PROJECT_H = (0, 768)
OUTPUT_Z = (768, 1024)
OUTPUT_H = (1024, 1280)
EPSILON = 1e-05
NEGATIVE = -1e30
SCALE = HEAD ** (-0.5)
LOG2E = 1.4426950408889634
QBLOCK = PATCH
MICRO = 1_150_000_000

F32 = jnp.float32
BF16 = jnp.bfloat16
PTS = ("x", "zh", "zl", "core")
GROUP = ("zl", "core")
ACROSS = ("x", "zh")


def dot(a, b, ca=1, cb=0):
    return lax.dot_general(a, b, (((ca,), (cb,)), ((), ())), preferred_element_type=F32)


def normalize(values):
    center = values - jnp.mean(values, axis=1, keepdims=True)
    inverse = lax.rsqrt(jnp.mean(center * center, axis=1, keepdims=True) + EPSILON)
    return center * inverse, inverse


def normalize_back(grad, unit, inverse):
    middle = grad - jnp.mean(grad, axis=1, keepdims=True)
    return inverse * (middle - unit * jnp.mean(grad * unit, axis=1, keepdims=True))


def iota(shape, dim):
    return lax.broadcasted_iota(jnp.int32, shape, dim)


def call(kernel, ins, outs, scratch=(), limit=32, micros=1, pull=False):
    views = [item[1:] if isinstance(item, tuple) else None for item in ins]
    arrays = [item[0] if isinstance(item, tuple) else item for item in ins]
    scalars = [a.ndim == 1 for a in arrays]
    held = [pltpu.VMEM(a.shape, a.dtype) for a in arrays] if pull else []
    held += [pltpu.SemaphoreType.DMA((len(arrays),))] if pull else []

    def body(*refs):
        given = list(refs)
        if pull:
            given, buffers, sems = given[: -len(held)], given[-len(held) : -1], given[-1]
            copies = [
                pltpu.make_async_copy(refs[k], buffer, sems.at[k]) for k, buffer in enumerate(buffers)
            ]
            for copy in copies:
                copy.start()
            for copy in copies:
                copy.wait()
            given[: len(buffers)] = buffers
        for k, view in enumerate(views):
            if view is not None:
                lead = (slice(None),) * (len(arrays[k].shape) - 1)
                given[k] = refs[k].at[lead + (pl.ds(view[0], view[1] - view[0]),)]
        kernel(*given)

    return pl.pallas_call(
        body,
        out_shape=[jax.ShapeDtypeStruct(shape, dtype) for shape, dtype in outs],
        in_specs=[
            pl.BlockSpec(memory_space=pltpu.SMEM if flat else pl.ANY if pull else pltpu.VMEM)
            for flat in scalars
        ],
        out_specs=[pl.BlockSpec(memory_space=pltpu.VMEM) for _ in outs],
        scratch_shapes=list(scratch) + held,
        cost_estimate=pl.CostEstimate(flops=micros * MICRO, bytes_accessed=0, transcendentals=0),
        compiler_params=pltpu.CompilerParams(vmem_limit_bytes=limit * 1024 * 1024),
    )(*arrays)


def masked_scores(keys, query, mask):
    return jnp.where(mask, dot(keys, query, 1, 1) * (SCALE * LOG2E), NEGATIVE)


def softmax_keys(keys, query, mask):
    scores = masked_scores(keys, query, mask)
    highest = jnp.max(scores, axis=0, keepdims=True)
    weights = jnp.exp2(scores - highest)
    inverse = 1.0 / jnp.sum(weights, axis=0, keepdims=True)
    return weights * inverse, highest, inverse


def split_exact(values):
    parts = []
    for _ in range(3):
        part = values.astype(BF16).astype(F32)
        parts.append(part)
        values = values - part
    return parts


def key_mask(flags):
    parts = []
    for b in range(MEMBERS):
        pick = jnp.where(iota((MEMBERS, QBLOCK), 0) == b, 1.0, 0.0).astype(BF16)
        parts.append(dot(flags, pick, 0, 0))
    return jnp.concatenate(parts, axis=0) > 0.5


def place_rows(targets):
    patch = targets[...] // PATCH
    patches = jnp.broadcast_to(patch, (MEMBERS, ROWS)).astype(F32)
    column = jnp.broadcast_to(patches.T[:, :1], (ROWS, ROWS))
    row = jnp.broadcast_to(patch, (ROWS, ROWS)).astype(F32)
    same = (column == row) & (iota((ROWS, ROWS), 0) < iota((ROWS, ROWS), 1))
    rank = jnp.sum(jnp.where(same, 1.0, 0.0), axis=0, keepdims=True).astype(jnp.int32)
    code = patch * SLOTS + rank
    return jnp.where(iota((PATCHES * SLOTS, ROWS), 0) == code, 1.0, 0.0).astype(BF16)


def prepare_kernel(
    points, cotangent, targets, sources, project_z, project_h, output_z, output_h, mine, weights, grads
):
    grads[...] = dot(place_rows(targets), cotangent[...]).astype(BF16)
    mine[:ROWS, :] = points[...]
    source = sources[...]
    digits = jnp.concatenate([source // ROWS, source % ROWS], axis=1).astype(F32)
    digits = jnp.concatenate([digits, jnp.zeros((1, WIDTH - 2 * ROWS), F32)], axis=1)
    mine[ROWS:, :] = jnp.broadcast_to(digits, (META, WIDTH)).astype(BF16)
    for c in range(2):
        pieces = []
        for project in (project_z, project_h):
            values = project[...].astype(F32)
            pairs = range(c, MEMBERS, 2)
            pieces += [values[:, k * PAIR : (k + 1) * PAIR] for k in pairs]
            for k in pairs:
                pieces += [
                    values[:, n * WIDTH + k * PAIR : n * WIDTH + (k + 1) * PAIR] for n in (1, 2)
                ]
        for output in (output_z, output_h):
            half = WIDTH // 2
            pieces.append(output[:, c * half : (c + 1) * half].astype(F32))
        weights[c] = jnp.concatenate(pieces, axis=1).astype(BF16)


def forward_kernel(scal, gathered, own, one, two, three, qkv, attended, plan, att, weights):
    member = scal[0]
    limit = scal[2 + scal[1]]
    for k, part in enumerate((own, one, two, three)):
        place = jnp.bitwise_xor(scal[1] // 4, k)
        weights[pl.ds(pl.multiple_of(place * ROWS, ROWS), ROWS), :] = part[...]
    w = weights[...]
    stride = ROWS + META
    source = gathered
    device = iota((ROWS, ROWS), 0)
    total = jnp.zeros((ROWS, ROWS), F32)
    flagged = jnp.zeros((ROWS, ROWS), F32)
    bound = jnp.concatenate(
        [scal[2 + k] - ROWS * iota((MEMBERS, ROWS), 0) for k in range(PATCHES)], axis=0
    ).astype(F32)
    device_f = device.astype(F32)
    for b in range(MEMBERS):
        first = b * stride
        block = source[first : first + ROWS, :]
        unit, _ = normalize(block.astype(F32))
        unit = unit.astype(BF16)
        rows = slice(b * ROWS, (b + 1) * ROWS)
        qkv[rows, :] = dot(unit, w).astype(BF16)
        meta = source[first + ROWS : first + stride, :].astype(F32)
        owner = meta[0:1, 0:ROWS]
        place = meta[0:1, ROWS : 2 * ROWS]
        hit = device_f == owner
        total += jnp.where(hit, 1.0, 0.0)
        flagged += jnp.where(hit & (place < bound), 1.0, 0.0)
    total = jnp.sum(total, axis=1, keepdims=True)
    flagged = jnp.sum(flagged, axis=1, keepdims=True)
    lane = iota((MEMBERS, ROWS), 1).astype(F32)
    mine = iota((MEMBERS, 1), 0) == member
    slot = iota((SLOTS, ROWS), 0).astype(F32)
    lane_slot = iota((SLOTS, ROWS), 1).astype(F32)
    offset = jnp.zeros((MEMBERS, 1), F32)
    flags = jnp.zeros((MEMBERS, ROWS), F32)
    for k in range(PATCHES):
        here = total[k * MEMBERS : (k + 1) * MEMBERS, :]
        good = flagged[k * MEMBERS : (k + 1) * MEMBERS, :]
        flags += jnp.where((lane >= offset) & (lane < offset + good), 1.0, 0.0)
        own_first = jnp.sum(jnp.where(mine, offset, 0.0), axis=0, keepdims=True)
        own_count = jnp.sum(jnp.where(mine, here, 0.0), axis=0, keepdims=True)
        plan[k * SLOTS : (k + 1) * SLOTS, :] = jnp.where(
            (slot + own_first == lane_slot) & (slot < own_count), 1.0, 0.0
        ).astype(BF16)
        offset += here
    plan[PATCHES * SLOTS :, :] = jnp.concatenate([flags, flags], axis=0).astype(BF16)
    mask = iota((PATCH, QBLOCK), 0) < limit
    norms = []
    for h in range(2):
        keys = qkv[:, h * HEAD : (h + 1) * HEAD]
        values_t = qkv[:, PAIR + h * HEAD : PAIR + (h + 1) * HEAD].astype(F32).T.astype(BF16)
        for n in range(PATCH // QBLOCK):
            span = slice(n * QBLOCK, (n + 1) * QBLOCK)
            query = qkv[span, 2 * PAIR + h * HEAD : 2 * PAIR + (h + 1) * HEAD]
            probs, highest, inverse = softmax_keys(keys, query, mask)
            norms += split_exact(highest) + split_exact(inverse)
            att[h * HEAD : (h + 1) * HEAD, span] = dot(values_t, probs.astype(BF16))
    norms.append(jnp.zeros((PAIR - 12, PATCH), F32))
    qkv[:, 3 * PAIR :] = jnp.concatenate(norms, axis=0).T.astype(BF16)
    for b in range(MEMBERS):
        attended[b] = att[:, b * ROWS : (b + 1) * ROWS].astype(BF16)


def halves(blocks, first, last):
    return [
        jnp.concatenate([blocks[2 * x + c, :, first:last] for x in range(4)], axis=0)
        for c in range(2)
    ]


def mix_kernel(targets, attended, points, shared, send):
    place = place_rows(targets)
    weights = halves(shared, 0, WIDTH // 2)
    mixed = jnp.concatenate([dot(attended[...], w, 0, 0) for w in weights], axis=1)
    mixed = points[...].astype(F32) + mixed
    send[...] = dot(place, mixed.astype(BF16)).astype(BF16)


def collect_kernel(arrived, plan, grads):
    grads[...] = dot(plan[: PATCHES * SLOTS, :], arrived[...], 0, 0).astype(BF16)


def project_kernel(arrived, plan, project, output, grads, send, rows):
    mixed = dot(plan[: PATCHES * SLOTS, :], arrived[...], 0, 0).astype(BF16)
    rows[...] = mixed
    low, high = halves(output, 0, WIDTH // 2)
    grad_attended = dot(grads[:, : WIDTH // 2], low, 1, 1) + dot(grads[:, WIDTH // 2 :], high, 1, 1)
    unit, _ = normalize(mixed.astype(F32))
    unit = unit.astype(BF16)
    projected = [dot(unit, w) for w in halves(project, 0, 3 * WIDTH // 2)]
    for k in range(MEMBERS):
        half, t = projected[k % 2], k // 2
        first = WIDTH // 2 + t * 2 * PAIR
        send[k, :ROWS, :] = half[:, first : first + 2 * PAIR].astype(BF16)
        send[k, ROWS:, :] = jnp.concatenate(
            [half[:, t * PAIR : (t + 1) * PAIR], grad_attended[:, k * PAIR : (k + 1) * PAIR]],
            axis=1,
        ).astype(BF16)


def backward_body(qkv, grad_t, mask, norms, send, attended, dq, dk, dv):
    for h in range(2):
        low, high = h * HEAD, (h + 1) * HEAD
        keys = qkv[:, low:high]
        values = qkv[:, PAIR + low : PAIR + high]
        keys_t = keys.astype(F32).T.astype(BF16)
        values_t = values.astype(F32).T.astype(BF16)
        for n in range(PATCH // QBLOCK):
            span = slice(n * QBLOCK, (n + 1) * QBLOCK)
            query = qkv[span, 2 * PAIR + low : 2 * PAIR + high]
            grad = grad_t[low:high, span]
            if norms is None:
                probs, _, _ = softmax_keys(keys, query, mask)
            else:
                weights = jnp.exp2(masked_scores(keys, query, mask) - norms[2 * h][:, span])
                probs = weights * norms[2 * h + 1][:, span]
            probs_low = probs.astype(BF16)
            grad_probs = dot(values, grad)
            row_dot = jnp.sum(probs * grad_probs, axis=0, keepdims=True)
            grad_scores = (probs * (grad_probs - row_dot)).astype(BF16)
            dq[low:high, span] = dot(keys_t, grad_scores)
            part_k = dot(grad_scores, query)
            part_v = dot(probs_low, grad, 1, 1)
            if n == 0:
                dk[:, low:high] = part_k
                dv[:, low:high] = part_v
            else:
                dk[:, low:high] += part_k
                dv[:, low:high] += part_v
            if attended is not None:
                attended[low:high, span] = dot(values_t, probs_low).astype(BF16)
    for b in range(MEMBERS):
        rows = slice(b * ROWS, (b + 1) * ROWS)
        send[b, :ROWS, :] = jnp.concatenate([dk[rows, :] * SCALE, dv[rows, :]], axis=1).astype(BF16)
        send[b, ROWS:, :] = (dq[:, rows] * SCALE).astype(BF16)


def backward_h_kernel(arrived, plan, send, attended, qkv, grad_t, dq, dk, dv):
    for b in range(MEMBERS):
        rows = slice(b * ROWS, (b + 1) * ROWS)
        qkv[rows, :ROWS] = arrived[b, :ROWS, :]
        both = arrived[b, ROWS:, :]
        qkv[rows, ROWS:] = both
        grad_t[:, rows] = both.astype(F32).T[PAIR:, :].astype(BF16)
    mask = key_mask(plan[PATCHES * SLOTS : PATCHES * SLOTS + MEMBERS, :])
    backward_body(qkv, grad_t, mask, None, send, attended, dq, dk, dv)


def backward_z_kernel(scal, arrived, qkv, send, grad_t, dq, dk, dv):
    for b in range(MEMBERS):
        grad_t[:, b * ROWS : (b + 1) * ROWS] = arrived[b]
    mask = iota((PATCH, QBLOCK), 0) < scal[2 + scal[1]]
    kept = qkv[:, 3 * PAIR :].astype(F32).T
    norms = [kept[k : k + 1, :] + kept[k + 1 : k + 2, :] + kept[k + 2 : k + 3, :] for k in (0, 3, 6, 9)]
    backward_body(qkv, grad_t, mask, norms, send, None, dq, dk, dv)


def input_grad(arrived, weights, rows, grads):
    sides = []
    for c in range(2):
        members = range(c, MEMBERS, 2)
        query_part = jnp.concatenate([arrived[k, ROWS:, :].astype(F32) for k in members], axis=0)
        sides.append(
            jnp.concatenate(
                [query_part.T.astype(BF16)] + [arrived[k, :ROWS, :] for k in members], axis=1
            )
        )
    grad_normed = dot(sides[0], weights[0], 1, 1) + dot(sides[1], weights[1], 1, 1)
    unit, inverse = normalize(rows[...].astype(F32))
    return (grads[...].astype(F32) + normalize_back(grad_normed, unit, inverse)).astype(BF16)


def return_kernel(arrived, project, rows, grads, plan, attended, all_grads, send):
    grad = input_grad(arrived, halves(project, 0, 3 * WIDTH // 2), rows, grads)
    spaced = dot(plan[: PATCHES * SLOTS, :], grad).astype(BF16)
    term = dot(attended[...], all_grads[...]).astype(BF16)
    tiles = [slice(t * ROWS, (t + 1) * ROWS) for t in range(4)]
    for k in range(PATCHES):
        rows = spaced[k * SLOTS : (k + 1) * SLOTS, :]
        for t, tile in enumerate(tiles):
            send[k, t * SLOTS : (t + 1) * SLOTS, :] = rows[:, tile]
        share = term[k * SHARE : (k + 1) * SHARE, :]
        send[k, 4 * SLOTS :, :] = jnp.concatenate([share[:, tile] for tile in tiles], axis=0)


def regain_kernel(arrived, targets, output, grad_mixed, send, term):
    spaced = jnp.concatenate(
        [
            jnp.concatenate([arrived[k, t * SLOTS : (t + 1) * SLOTS, :] for k in range(PATCHES)], axis=0)
            for t in range(4)
        ],
        axis=1,
    )
    grad = dot(place_rows(targets), spaced, 0, 0).astype(BF16)
    grad_mixed[...] = grad
    low, high = halves(output, 0, WIDTH // 2)
    grad_attended = dot(low, grad[:, : WIDTH // 2], 1, 1) + dot(high, grad[:, WIDTH // 2 :], 1, 1)
    send[...] = grad_attended.astype(BF16)
    total = jnp.zeros((4 * SHARE, ROWS), F32)
    for k in range(PATCHES):
        total += arrived[k, 4 * SLOTS :, :].astype(F32)
    total = jnp.concatenate([total[t * SHARE : (t + 1) * SHARE, :] for t in range(4)], axis=1)
    term[...] = total * (SCENES * PATCHES * PATCH) ** (-0.5)


def finish_kernel(arrived, project, rows, grads, out):
    out[...] = input_grad(arrived, halves(project, 0, 3 * WIDTH // 2), rows, grads)


def exchange(value, axes):
    return lax.all_to_all(value, axes, split_axis=0, concat_axis=0, tiled=True)


def per_device(
    points, cotangent, valid_counts, zorder_targets, hilbert_sources,
    zorder_project, zorder_output, hilbert_project, hilbert_output,
):
    rows = points[0]
    cot = cotangent[0]
    member = lax.axis_index(GROUP).astype(jnp.int32)
    patch = lax.axis_index(ACROSS).astype(jnp.int32)
    scal = jnp.concatenate([jnp.stack([member, patch]), valid_counts[0]])
    targets = zorder_targets[0]
    sources = hilbert_sources[0]

    targets = targets[None, :]
    mine, weights, send_grads = call(
        prepare_kernel,
        [rows, cot, targets, sources[None, :], zorder_project, hilbert_project, zorder_output, hilbert_output],
        [
            ((ROWS + META, WIDTH), BF16),
            ((2, SHARE, 4 * WIDTH), BF16),
            ((PATCHES * SLOTS, WIDTH), BF16),
        ],
        limit=60,
        pull=True,
    )
    gathered = lax.all_gather(mine, GROUP, axis=0, tiled=True)
    weights = exchange(weights, "core").reshape(MEMBERS, 4 * WIDTH)
    weights = lax.all_gather(weights, ("zh", "zl"), axis=0, tiled=True)
    third = 3 * WIDTH // 2
    quarter = lax.axis_index("zl")
    own = jnp.concatenate(
        [
            lax.dynamic_slice_in_dim(weights, 4 * PAIR + quarter * 2 * PAIR, 2 * PAIR, 1),
            lax.dynamic_slice_in_dim(weights, quarter * PAIR, PAIR, 1),
            jnp.zeros((ROWS, PAIR), BF16),
        ],
        axis=1,
    )
    shared = lax.all_gather(weights[:, third:], ("x", "core"), axis=0, tiled=True)
    shared = shared.reshape(MEMBERS, ROWS, third + WIDTH)
    project_z = weights[:, :third]

    send_grads, own, gathered = lax.optimization_barrier((send_grads, own, gathered))
    others = [lax.ppermute(own, "x", [(i, i ^ k) for i in range(4)]) for k in (1, 2, 3)]
    arrived_grads = exchange(send_grads.reshape(PATCHES, SLOTS, WIDTH), ACROSS)

    qkv_z, attended, plan = call(
        forward_kernel,
        [scal, gathered, own] + others,
        [
            ((PATCH, 4 * PAIR), BF16),
            ((MEMBERS, PAIR, ROWS), BF16),
            ((PATCHES * SLOTS + 2 * MEMBERS, ROWS), BF16),
        ],
        [pltpu.VMEM((PAIR, PATCH), F32), pltpu.VMEM((WIDTH, 4 * PAIR), BF16)],
        micros=8,
    )

    attended, arrived_grads, project_z = lax.optimization_barrier((attended, arrived_grads, project_z))
    project_z = lax.all_gather(project_z, ("x", "core"), axis=0, tiled=True)
    project_z = project_z.reshape(MEMBERS, ROWS, third)
    (grads_h,) = call(
        collect_kernel,
        [arrived_grads.reshape(PATCHES * SLOTS, WIDTH), plan],
        [((ROWS, WIDTH), BF16)],
    )
    attended = exchange(attended, GROUP).reshape(WIDTH, ROWS)
    attended, grads_h, shared = lax.optimization_barrier((attended, grads_h, shared))
    all_grads_h = lax.all_gather(grads_h, GROUP, axis=0, tiled=True)
    (send,) = call(
        mix_kernel,
        [targets, attended, rows, (shared, *OUTPUT_Z)],
        [((PATCHES * SLOTS, WIDTH), BF16)],
    )

    arrived = exchange(send.reshape(PATCHES, SLOTS, WIDTH), ACROSS)
    send, rows_h = call(
        project_kernel,
        [
            arrived.reshape(PATCHES * SLOTS, WIDTH),
            plan,
            (shared, *PROJECT_H),
            (shared, *OUTPUT_H),
            grads_h,
        ],
        [((MEMBERS, 2 * ROWS, ROWS), BF16), ((ROWS, WIDTH), BF16)],
    )

    arrived = exchange(send, GROUP)
    sums = [
        pltpu.VMEM((PAIR, PATCH), F32),
        pltpu.VMEM((PATCH, PAIR), F32),
        pltpu.VMEM((PATCH, PAIR), F32),
    ]
    send, attended_h = call(
        backward_h_kernel,
        [arrived, plan],
        [((MEMBERS, 3 * PAIR, ROWS), BF16), ((PAIR, PATCH), BF16)],
        [pltpu.VMEM((PATCH, 4 * PAIR), BF16), pltpu.VMEM((PAIR, PATCH), BF16)] + sums,
        micros=11,
    )

    arrived = exchange(send, GROUP)
    (send,) = call(
        return_kernel,
        [arrived, (shared, *PROJECT_H), rows_h, grads_h, plan, attended_h, all_grads_h],
        [((PATCHES, 4 * SLOTS + 4 * SHARE, ROWS), BF16)],
    )

    arrived = exchange(send, ACROSS)
    grad_mixed, send, term = call(
        regain_kernel,
        [arrived, targets, (shared, *OUTPUT_Z)],
        [((ROWS, WIDTH), BF16), ((WIDTH, ROWS), BF16), ((SHARE, WIDTH), F32)],
    )
    term = lax.ppermute(
        term,
        PTS,
        [(r * MEMBERS + j, j * PATCHES + r) for r in range(PATCHES) for j in range(MEMBERS)],
    )
    arrived = exchange(send.reshape(MEMBERS, PAIR, ROWS), GROUP)
    (send,) = call(
        backward_z_kernel,
        [scal, arrived, qkv_z],
        [((MEMBERS, 3 * PAIR, ROWS), BF16)],
        [pltpu.VMEM((PAIR, PATCH), BF16)] + sums,
        micros=11,
    )
    send, term = lax.optimization_barrier((send, term))
    for k in (1, 2):
        term = term + lax.ppermute(term, "scene", [(i, i ^ k) for i in range(SCENES)])

    arrived = exchange(send, GROUP)
    (out,) = call(finish_kernel, [arrived, project_z, rows, grad_mixed], [((ROWS, WIDTH), BF16)])
    return out[None], term


def solution(mesh):
    devices = mesh.devices.reshape(4, 4, 4, 2, 4)
    fine = Mesh(devices, ("x", "zh", "zl", "core", "scene"))
    rows = P("scene", PTS, None)
    index = P("scene", PTS)
    weight = P(PTS, None)
    return jax.shard_map(
        per_device,
        mesh=fine,
        in_specs=(rows, rows, P("scene", None), index, index, weight, weight, weight, weight),
        out_specs=(rows, weight),
        check_vma=False,
    )
```
